128 devices in a mesh: dp: 4 (over x), ctx: 32 (over y, z, core).
Axes of the slice: x: 4, y: 4, z: 4, core: 2. Of those that a mesh axis runs over, the one named last changes fastest.
Arguments:
- query_states: bfloat16 [4, 4096, 2048], P('dp', 'ctx'), may hold values from -24 to 24
- key_states: bfloat16 [4, 4096, 1024], P('dp', 'ctx'), may hold values from -6 to 6
- value_states: bfloat16 [4, 4096, 1024], P('dp', 'ctx'), may hold values from -6 to 6
- out_grads: bfloat16 [4, 4096, 2048], P('dp', 'ctx'), may hold values from -6 to 6
- image_counts: int32 [4], P('dp'), may hold values from 256 to 2048, as said below
- prefix_lengths: int32 [4], P('dp'), may hold values from 257 to 3072, as said below
- encoder_owner: int32 [4], replicated, may hold values from 0 to 3, each once
- key_weight: bfloat16 [4608, 1024], replicated, may hold values from -0.09375 to 0.09375
- value_weight: bfloat16 [4608, 1024], replicated, may hold values from -0.09375 to 0.09375
- norm_scale: float32 [4608], P('dp'), may hold values from 0.5 to 2
- image_embed: bfloat16 [4, 2048, 4608], P(None, 'ctx', 'dp'), may hold values from -1200 to 1200
Outputs:
- query_grads: bfloat16 [4, 4096, 2048], P('dp', 'ctx')
- key_grads: bfloat16 [4, 4096, 1024], P('dp', 'ctx')
- value_grads: bfloat16 [4, 4096, 1024], P('dp', 'ctx')
- image_grads: float32 [4, 2048, 4608], P(None, 'ctx', 'dp')
The draws below stay inside these ranges and needn't reach their ends.
Inputs may be any that keep to these rules, and one draw needn't show every extreme that they name: `image_counts`: in every draw one sample has exactly 2048 image tokens and another exactly 256. `prefix_lengths`: each is at least one more than its sample's image_counts; in every draw one reaches 3072.
All inputs are finite; a program needn't handle non-finite values.
Results may differ from the reference program's by a relative error of at most 0.02.
Values may be sent and summed in bfloat16 or wider, within the bound.
No kernel may reach another device: no remote copies, remote signals or barrier semaphores. Data moves between devices by JAX's collectives and lax.ppermute only.
A program may use at most 192 MiB of HBM per device.

```python
import math
import jax
import jax.numpy as jnp
from jax import lax

D = 4608
H = 16
KVH = 8
HD = 128
TOK_DEV = 128
BATCH = 4
SEQ = 4096
QF = 2048
KVF = 1024
ENC_DEV = 64
IMG_MOST = 2048
IMG_LEAST = 256


def lengths_pair(key):
    places = jnp.arange(BATCH)
    chosen = jax.random.randint(jax.random.fold_in(key, 12), (), 0, BATCH)
    counts = jax.random.randint(jax.random.fold_in(key, 11), (BATCH,), IMG_LEAST, IMG_MOST + 1)
    counts = jnp.where(places == chosen, IMG_MOST, counts)
    counts = jnp.where(places == (chosen + 1) % BATCH, IMG_LEAST, counts)
    prompt = jax.random.randint(jax.random.fold_in(key, 13), (BATCH,), 1, SEQ // 4 + 1)
    prompt = jnp.where(places == chosen, SEQ // 4, prompt)
    prompt = jnp.where(places == (chosen + 1) % BATCH, 1, prompt)
    return (counts.astype(jnp.int32), (counts + prompt).astype(jnp.int32))


def draw_image_counts(key, part):
    counts, prefix = lengths_pair(key)
    return counts


def draw_prefix_lengths(key, part):
    counts, prefix = lengths_pair(key)
    return prefix


def draw_image_embed(key, part):
    key = jax.random.fold_in(key, 5)
    base_key, row_key, col_key = jax.random.split(key, 3)
    base = jnp.clip(jax.random.normal(base_key, (BATCH, IMG_MOST, D), jnp.float32), -4.0, 4.0)
    row_top = 10.0
    rows = jnp.exp(jax.random.uniform(row_key, (BATCH, IMG_MOST, 1), jnp.float32, 0.0, math.log(row_top)))
    ramp = math.log(3.0) * jnp.arange(D).astype(jnp.float32) / (D - 1)
    cols = jnp.exp(ramp[None, None, :] + jax.random.uniform(col_key, (1, 1, D), jnp.float32, 0.0, math.log(10.0)))
    return (base * rows * cols).astype(jnp.bfloat16)


def steps_of(key, dims, pieces, least, largest):
    factor_of = 1.0
    for axis_at, shards_of in pieces:
        draws = jax.random.uniform(jax.random.fold_in(jax.random.fold_in(key, 6), axis_at), (shards_of,), jnp.float32, least / len(pieces), largest / len(pieces))
        factor_of = factor_of * jnp.repeat(jnp.exp(draws), dims[axis_at] // shards_of).reshape((-1,) + (1,) * (len(dims) - 1 - axis_at))
    return factor_of


def scatter_about(key, extent, width, reach, pieces=(), kind=jnp.bfloat16):
    drawn = jax.random.normal(key, extent, jnp.float32) * width
    if len(pieces) > 0:
        drawn = steps_of(key, extent, pieces, -0.22, 0.18) * drawn
    return jnp.clip(drawn, min=-reach, max=reach).astype(kind)


def setup_inputs(seed: int = 0) -> dict:
    key_of = jax.random.split(jax.random.key(seed), 12)
    query_states = scatter_about(key_of[0], (BATCH, SEQ, QF), 4.0, 24.0, ((0, 4), (1, 32)))
    key_states = scatter_about(key_of[1], (BATCH, SEQ, KVF), 1.0, 6.0, ((0, 4), (1, 32)))
    value_states = scatter_about(key_of[2], (BATCH, SEQ, KVF), 1.0, 6.0, ((0, 4), (1, 32)))
    out_grads = scatter_about(key_of[3], (BATCH, SEQ, QF), 1.0, 6.0, ((0, 4), (1, 32)))
    image_counts = draw_image_counts(jax.random.fold_in(key_of[11], 71), 0)
    prefix_lengths = draw_prefix_lengths(jax.random.fold_in(key_of[11], 71), 0)
    encoder_owner = jax.random.permutation(key_of[6], BATCH).astype(jnp.int32)
    key_weight = scatter_about(key_of[7], (D, KVF), D ** -0.5, 0.09375)
    value_weight = scatter_about(key_of[8], (D, KVF), D ** -0.5, 0.09375)
    norm_scale = jnp.clip(jnp.exp(math.log(2.0) - 1.3862944 * jax.random.uniform(key_of[9], (D,), jnp.float32) ** steps_of(key_of[9], (D,), ((0, 4),), -0.2, 0.2)), 0.5, 2.0)
    image_embed = draw_image_embed(jax.random.fold_in(key_of[11], 71), 0)
    return dict(query_states=query_states, key_states=key_states, value_states=value_states, out_grads=out_grads, image_counts=image_counts, prefix_lengths=prefix_lengths, encoder_owner=encoder_owner, key_weight=key_weight, value_weight=value_weight, norm_scale=norm_scale, image_embed=image_embed)


score_scale = 144.0 ** (-0.5)
soft_cap = 50.0
norm_eps = 1e-06

def head_group(query_grp, key_head, value_head, grad_grp, prefix):
    positions = jnp.arange(SEQ)
    visible = (positions[None, :] < prefix) | (positions[None, :] <= positions[:, None])
    raw_scores = jnp.einsum('gqd,kd->gqk', query_grp, key_head) * score_scale
    squashed = jnp.tanh(raw_scores / soft_cap)
    capped = soft_cap * squashed
    unnormed = jnp.where(visible[None], jnp.exp(capped), 0.0)
    log_total = jnp.log(lax.optimization_barrier(jnp.sum(unnormed, -1, keepdims=True)))
    soft_probs = jnp.where(visible[None], jnp.exp(capped - log_total), 0.0)
    prob_grads = jnp.einsum('gqd,kd->gqk', grad_grp, value_head)
    row_delta = lax.optimization_barrier(jnp.sum(soft_probs * prob_grads, -1, keepdims=True))
    weight_grad = (score_scale * soft_probs * (prob_grads - row_delta) * (1.0 - squashed * squashed)).astype(jnp.bfloat16)
    weight_real = lax.optimization_barrier(weight_grad).astype(jnp.float32)
    probs_real = lax.optimization_barrier(soft_probs.astype(jnp.bfloat16)).astype(jnp.float32)
    query_part = jnp.einsum('gqk,kd->gqd', weight_real, key_head)
    blocks = SEQ // TOK_DEV
    group_size = query_grp.shape[0]
    weight_blocks = weight_real.reshape(group_size, blocks, TOK_DEV, SEQ)
    probs_blocks = probs_real.reshape(group_size, blocks, TOK_DEV, SEQ)
    query_blocks = query_grp.reshape(group_size, blocks, TOK_DEV, HD)
    grad_blocks = grad_grp.reshape(group_size, blocks, TOK_DEV, HD)
    key_terms = jnp.einsum('gnqk,gnqd->nkd', weight_blocks, query_blocks).astype(jnp.bfloat16)
    value_terms = jnp.einsum('gnqk,gnqd->nkd', probs_blocks, grad_blocks).astype(jnp.bfloat16)
    key_part = lax.optimization_barrier(jnp.sum(lax.optimization_barrier(key_terms).astype(jnp.float32), 0))
    value_part = lax.optimization_barrier(jnp.sum(lax.optimization_barrier(value_terms).astype(jnp.float32), 0))
    return (query_part, key_part, value_part)

def reference(query_states, key_states, value_states, out_grads, image_counts, prefix_lengths, encoder_owner, key_weight, value_weight, norm_scale, image_embed):
    group_size = H // KVH
    query_list = []
    key_list = []
    value_list = []
    for sample in range(BATCH):
        queries = query_states[sample].astype(jnp.float32).reshape(SEQ, KVH, group_size, HD).transpose(1, 2, 0, 3)
        key_heads = key_states[sample].astype(jnp.float32).reshape(SEQ, KVH, HD).transpose(1, 0, 2)
        value_heads = value_states[sample].astype(jnp.float32).reshape(SEQ, KVH, HD).transpose(1, 0, 2)
        grad_heads = out_grads[sample].astype(jnp.float32).reshape(SEQ, KVH, group_size, HD).transpose(1, 2, 0, 3)
        prefix = prefix_lengths[sample]

        def per_head(items):
            return head_group(items[0], items[1], items[2], items[3], prefix)
        query_part, key_part, value_part = lax.map(per_head, (queries, key_heads, value_heads, grad_heads))
        query_list.append(query_part.transpose(2, 0, 1, 3).reshape(SEQ, H * HD).astype(jnp.bfloat16))
        key_list.append(key_part.transpose(1, 0, 2).reshape(SEQ, KVH * HD).astype(jnp.bfloat16))
        value_list.append(value_part.transpose(1, 0, 2).reshape(SEQ, KVH * HD).astype(jnp.bfloat16))
    query_grads = jnp.stack(query_list)
    key_grads = jnp.stack(key_list)
    value_grads = jnp.stack(value_list)
    slot_index = jnp.arange(IMG_MOST)
    token_of = (slot_index % ENC_DEV * (SEQ // TOK_DEV) + slot_index // ENC_DEV).astype(jnp.int32)
    rows_list = []
    for sample in range(BATCH):
        key_rows = jnp.take(key_grads[sample], token_of, axis=0)
        value_rows = jnp.take(value_grads[sample], token_of, axis=0)
        projected = jnp.dot(key_rows, key_weight.T, preferred_element_type=jnp.float32)
        projected = projected + jnp.dot(value_rows, value_weight.T, preferred_element_type=jnp.float32)
        projected = jnp.where((token_of < image_counts[sample])[:, None], projected, 0.0)
        rows_list.append(projected.astype(jnp.bfloat16))
    by_sample = jnp.stack(rows_list)
    samples = jnp.arange(BATCH).astype(jnp.int32)
    inverse = lax.optimization_barrier(jnp.sum(samples[:, None] * (encoder_owner[:, None] == samples[None, :]).astype(jnp.int32), 0)).astype(jnp.int32)
    embed_grad = jnp.take(by_sample, inverse, axis=0)
    embed_grad = lax.optimization_barrier(embed_grad).astype(jnp.float32)
    embed_rows = image_embed.astype(jnp.float32)
    inv_rms = lax.rsqrt(lax.optimization_barrier(jnp.mean(embed_rows * embed_rows, -1, keepdims=True)) + norm_eps)
    scaled = norm_scale * embed_grad
    image_grads = inv_rms * scaled - embed_rows * (inv_rms * inv_rms * inv_rms) * lax.optimization_barrier(jnp.mean(embed_rows * scaled, -1, keepdims=True))
    return (query_grads, key_grads, value_grads, image_grads)
```

```python
import functools
import math

import jax
import jax.numpy as jnp
from jax import lax
from jax.experimental import pallas as pl
from jax.experimental.pallas import tpu as pltpu
from jax.sharding import Mesh, PartitionSpec as P

D = 4608
HD = 128
KVH = 8
TOK = 128
SLOTS = 64
NDP = 4
FS = D // NDP
SEG = 512
NSEG = 8

score_scale = 144.0 ** (-0.5)
soft_cap = 50.0
norm_eps = 1e-06
tanh_scale = score_scale / soft_cap
exp2_scale = soft_cap * math.log2(math.e)

f32 = jnp.float32
bf16 = jnp.bfloat16
VM = pl.BlockSpec(memory_space=pltpu.VMEM)
SM = pl.BlockSpec(memory_space=pltpu.SMEM)
NT = (((1,), (1,)), ((), ()))
NN = (((1,), (0,)), ((), ()))


def mm(a, b, dims=NN):
    return lax.dot_general(a, b, dims, preferred_element_type=f32)


def split3(x):
    hi = x.astype(bf16)
    rest = x - hi.astype(f32)
    mid = rest.astype(bf16)
    lo = (rest - mid.astype(f32)).astype(bf16)
    return hi, mid, lo


def pack_kernel(width, a_ref, b_ref, out_ref):
    for h in range(KVH):
        out_ref[h, :, :width] = a_ref[:, h * width : (h + 1) * width]
        out_ref[h, :, width:] = b_ref[:, h * width : (h + 1) * width]


def pack_heads(a, b, name):
    width = a.shape[1] // KVH
    return pl.pallas_call(
        functools.partial(pack_kernel, width),
        out_shape=jax.ShapeDtypeStruct((KVH, TOK, 2 * width), bf16),
        in_specs=[VM, VM],
        out_specs=VM,
        name=name,
    )(a, b)


def embed_pack_kernel(owner_ref, embed_ref, scale_ref, out_ref):
    out_ref[0, :SLOTS, :] = embed_ref[0]
    row = lax.broadcasted_iota(jnp.int32, (16, FS), 0)
    hi, mid, lo = split3(scale_ref[...])
    parts = jnp.where(row == 0, hi.astype(f32), jnp.where(row == 1, mid.astype(f32), 0.0))
    parts = jnp.where(row == 2, lo.astype(f32), parts)
    out_ref[0, SLOTS:, :] = parts.astype(bf16)


def pack_embed(owner, embed, scale):
    return pl.pallas_call(
        embed_pack_kernel,
        out_shape=jax.ShapeDtypeStruct((NDP, SLOTS + 16, FS), bf16),
        grid_spec=pltpu.PrefetchScalarGridSpec(
            num_scalar_prefetch=1,
            grid=(NDP,),
            in_specs=[
                pl.BlockSpec((1, SLOTS, FS), lambda b, owner: (owner[b], 0, 0)),
                pl.BlockSpec((1, FS), lambda b, owner: (0, 0)),
            ],
            out_specs=pl.BlockSpec((1, SLOTS + 16, FS), lambda b, owner: (b, 0, 0)),
        ),
        name="pack_embed",
    )(owner, embed, scale)


def attention_kernel(
    sc_ref,
    qd_ref,
    kv0_ref,
    kv1_ref,
    kv2_ref,
    kv3_ref,
    dq_ref,
    own_ref,
    core_ref,
    far_ref,
    farcore_ref,
    tok_ref,
    k_s,
    v_s,
    kt_s,
    q_s,
    do_s,
    e_s,
    w_s,
    p_s,
    dk_s,
    dv_s,
    tot,
    mom,
    dqt,
    perm,
):
    prefix, zh, core = sc_ref[0], sc_ref[1], sc_ref[2]
    eye = (
        lax.broadcasted_iota(jnp.int32, (HD, HD), 0) == lax.broadcasted_iota(jnp.int32, (HD, HD), 1)
    ).astype(bf16)
    for seg in range(NSEG):
        near, away = ((kv0_ref, kv1_ref), (kv2_ref, kv3_ref))[seg // 4]
        y = seg % 4
        whole = jnp.concatenate([near[2 * y], near[2 * y + 1], away[2 * y], away[2 * y + 1]], 0)
        k_s[seg] = whole[:, :HD]
        v_s[seg] = whole[:, HD:]
        kt_s[seg] = mm(eye, whole[:, :HD], NT).astype(bf16)
    dk_s[...] = jnp.zeros_like(dk_s)
    dv_s[...] = jnp.zeros_like(dv_s)

    def key_start(j):
        far = j // 4
        return (j % 4) * 1024 + (zh + far - 2 * zh * far) * SEG

    def hidden(key0, row0):
        s = lax.broadcasted_iota(jnp.int32, (SEG, SEG), 0)
        piece = s // TOK
        other = piece // 2
        key = key0 + (piece % 2) * 256 + (core + other - 2 * core * other) * TOK + s % TOK
        lane = lax.broadcasted_iota(jnp.int32, (1, SEG), 1)
        row = row0 + ((lane // TOK) % 2) * 256 + lane % TOK
        return key >= jnp.maximum(row + 1, prefix)

    def row_body(i, _):
        row0 = i * 1024 + zh * SEG + core * TOK
        limit = jnp.maximum(prefix, row0 + 384)
        full = jnp.maximum(prefix, row0 + 1)
        for head in range(2):
            for z in range(2):
                at = pl.ds((head * 2 + z) * TOK, TOK)
                q_s[at, :] = qd_ref[2 * i + z, :, head * HD : (head + 1) * HD]
                do_s[at, :] = qd_ref[2 * i + z, :, (2 + head) * HD : (3 + head) * HD]
        tot[...] = jnp.zeros_like(tot)
        mom[...] = jnp.zeros_like(mom)
        dqt[...] = jnp.zeros_like(dqt)

        def scores(j, key0, masked):
            t = jnp.tanh(mm(k_s[j], q_s[...], NT) * tanh_scale)
            e = jnp.exp2(t * exp2_scale)
            if masked:
                e = jnp.where(hidden(key0, row0), 0.0, e)
            dp = mm(v_s[j], do_s[...], NT)
            tot[...] += jnp.sum(e, 0, keepdims=True)
            mom[...] += jnp.sum(e * dp, 0, keepdims=True)
            e_s[j] = e
            w_s[j] = e * (1.0 - t * t)
            p_s[j] = dp

        def first(j, _):
            key0 = key_start(j)

            @pl.when(key0 + SEG <= full)
            def _():
                scores(j, key0, False)

            @pl.when((key0 + SEG > full) & (key0 < limit))
            def _():
                scores(j, key0, True)

            return 0

        lax.fori_loop(0, NSEG, first, 0)
        inv = 1.0 / tot[...]
        delta = mom[...] * inv

        def second(j, _):
            @pl.when(key_start(j) < limit)
            def _():
                p = (e_s[j] * inv).astype(bf16)
                ds = (w_s[j] * inv * (p_s[j] - delta)).astype(bf16)
                dv_s[j] += mm(p, do_s[...])
                dk_s[j] += mm(ds, q_s[...])
                dqt[...] += mm(kt_s[j], ds)

            return 0

        lax.fori_loop(0, NSEG, second, 0)
        dq = (dqt[...] * score_scale).T.astype(bf16)
        for head in range(2):
            for z in range(2):
                at = (head * 2 + z) * TOK
                dq_ref[2 * i + z, :, head * HD : (head + 1) * HD] = dq[at : at + TOK]
        return 0

    lax.fori_loop(0, 4, row_body, 0)

    out = lax.broadcasted_iota(jnp.int32, (SEG, SEG), 0)
    src = lax.broadcasted_iota(jnp.int32, (SEG, SEG), 1)
    slot = out % 16
    c_of = (slot // 4) % 2
    want = (
        (c_of + core - 2 * c_of * core) * 256 + (slot // 8) * TOK + (slot % 4) * 32 + out // 16
    )
    perm[...] = (want == src).astype(bf16)
    for seg in range(NSEG):
        near, away = ((own_ref, core_ref), (far_ref, farcore_ref))[seg // 4]
        y = seg % 4
        terms = jnp.concatenate([dk_s[seg] * score_scale, dv_s[seg]], 1)
        near[2 * y] = terms[:TOK].astype(near.dtype)
        near[2 * y + 1] = terms[TOK : 2 * TOK].astype(near.dtype)
        away[2 * y] = terms[2 * TOK : 3 * TOK].astype(away.dtype)
        away[2 * y + 1] = terms[3 * TOK :].astype(away.dtype)
        if y < 2:
            moved = mm(perm[...], terms.astype(bf16)).astype(bf16).reshape(32, 16, 2 * HD)
            z_at = zh if seg < 4 else 1 - zh
            tok_ref[:, pl.ds(pl.multiple_of((2 * y + z_at) * 16, 16), 16), :] = moved


def attention(sc, qd, kv0, kv1, kv2, kv3):
    part = (KVH, TOK, 2 * HD)
    return pl.pallas_call(
        attention_kernel,
        out_shape=(
            jax.ShapeDtypeStruct(part, bf16),
            jax.ShapeDtypeStruct(part, f32),
            jax.ShapeDtypeStruct(part, bf16),
            jax.ShapeDtypeStruct(part, bf16),
            jax.ShapeDtypeStruct(part, bf16),
            jax.ShapeDtypeStruct((32, SLOTS, 2 * HD), bf16),
        ),
        in_specs=[SM] + [VM] * 5,
        out_specs=(VM,) * 6,
        scratch_shapes=[
            pltpu.VMEM((NSEG, SEG, HD), bf16),
            pltpu.VMEM((NSEG, SEG, HD), bf16),
            pltpu.VMEM((NSEG, HD, SEG), bf16),
            pltpu.VMEM((SEG, HD), bf16),
            pltpu.VMEM((SEG, HD), bf16),
            pltpu.VMEM((NSEG, SEG, SEG), f32),
            pltpu.VMEM((NSEG, SEG, SEG), f32),
            pltpu.VMEM((NSEG, SEG, SEG), f32),
            pltpu.VMEM((NSEG, SEG, HD), f32),
            pltpu.VMEM((NSEG, SEG, HD), f32),
            pltpu.VMEM((1, SEG), f32),
            pltpu.VMEM((1, SEG), f32),
            pltpu.VMEM((HD, SEG), f32),
            pltpu.VMEM((SEG, SEG), bf16),
        ],
        compiler_params=pltpu.CompilerParams(vmem_limit_bytes=58 << 20),
        cost_estimate=pl.CostEstimate(
            flops=20_000_000_000, bytes_accessed=8_000_000, transcendentals=16_000_000
        ),
        name="attention",
    )(sc, qd, kv0, kv1, kv2, kv3)


def pair_sum_kernel(a_ref, b_ref, out_ref):
    out_ref[...] = (a_ref[...].astype(f32) + b_ref[...].astype(f32)).astype(bf16)


def pair_sum(a, b):
    return pl.pallas_call(
        pair_sum_kernel,
        out_shape=jax.ShapeDtypeStruct(a.shape, bf16),
        in_specs=[VM, VM],
        out_specs=VM,
        name="pair_sum",
    )(a, b)


def last_sum_kernel(a_ref, b_ref, c_ref, out_ref):
    out_ref[...] = (a_ref[...] + b_ref[...].astype(f32) + c_ref[...].astype(f32)).astype(bf16)


def last_sum(a, b, c):
    return pl.pallas_call(
        last_sum_kernel,
        out_shape=jax.ShapeDtypeStruct(a.shape, bf16),
        in_specs=[VM] * 3,
        out_specs=VM,
        name="last_sum",
    )(a, b, c)


def unpack_kernel(dq_ref, dkv_ref, q_ref, k_ref, v_ref):
    for h in range(KVH):
        q_ref[:, h * 2 * HD : (h + 1) * 2 * HD] = dq_ref[h]
        k_ref[:, h * HD : (h + 1) * HD] = dkv_ref[h, :, :HD]
        v_ref[:, h * HD : (h + 1) * HD] = dkv_ref[h, :, HD:]


def unpack(dq, dkv):
    return pl.pallas_call(
        unpack_kernel,
        out_shape=(
            jax.ShapeDtypeStruct((TOK, 2 * KVH * HD), bf16),
            jax.ShapeDtypeStruct((TOK, KVH * HD), bf16),
            jax.ShapeDtypeStruct((TOK, KVH * HD), bf16),
        ),
        in_specs=[VM, VM],
        out_specs=(VM, VM, VM),
        name="unpack",
    )(dq, dkv)


def project_kernel(sc_ref, tok_ref, wk_ref, wv_ref, embed_ref, out_ref, xk_s, xv_s, sq, cross):
    step = pl.program_id(0)

    @pl.when(step == 0)
    def _():
        for h in range(KVH):
            base = (h // 2) * 8 + (h % 2) * 2
            total = tok_ref[base].astype(f32) + tok_ref[base + 1].astype(f32)
            total = total + tok_ref[base + 4].astype(f32) + tok_ref[base + 5].astype(f32)
            total = total.astype(bf16)
            xk_s[:, h * HD : (h + 1) * HD] = total[:, :HD]
            xv_s[:, h * HD : (h + 1) * HD] = total[:, HD:]
        sq[...] = jnp.zeros_like(sq)
        cross[...] = jnp.zeros_like(cross)

    projected = mm(xk_s[...], wk_ref[...], NT) + mm(xv_s[...], wv_ref[...], NT)
    token = lax.broadcasted_iota(jnp.int32, (SLOTS, FS), 0) * 32 + sc_ref[1]
    grad = jnp.where(token < sc_ref[0], projected, 0.0).astype(bf16)
    out_ref[step, :, :FS] = grad
    rows = embed_ref[0, :SLOTS, :].astype(f32)
    tail = embed_ref[0, SLOTS:, :].astype(f32)
    scale = tail[0:1] + tail[1:2] + tail[2:3]
    sq[...] += jnp.sum(rows * rows, 1, keepdims=True)
    cross[...] += jnp.sum(rows * (scale * grad.astype(f32)), 1, keepdims=True)

    @pl.when(step == NDP - 1)
    def _():
        lane = lax.broadcasted_iota(jnp.int32, (SLOTS, 128), 1)
        inv = lax.rsqrt(sq[...] / D + norm_eps)
        parts = split3(inv) + split3(cross[...] / D)
        tail = jnp.zeros((SLOTS, 128), f32)
        for n, part in enumerate(parts):
            tail = jnp.where(lane == n, part.astype(f32), tail)
        for n in range(NDP):
            out_ref[n, :, FS:] = tail.astype(bf16)


def project(sc, tok, wk, wv, embed):
    return pl.pallas_call(
        project_kernel,
        out_shape=jax.ShapeDtypeStruct((NDP, SLOTS, FS + 128), bf16),
        grid=(NDP,),
        in_specs=[
            SM,
            pl.BlockSpec((32, SLOTS, 2 * HD), lambda n: (0, 0, 0)),
            pl.BlockSpec((FS, KVH * HD), lambda n: (n, 0)),
            pl.BlockSpec((FS, KVH * HD), lambda n: (n, 0)),
            pl.BlockSpec((1, SLOTS + 16, FS), lambda n: (n, 0, 0)),
        ],
        out_specs=pl.BlockSpec((NDP, SLOTS, FS + 128), lambda n: (0, 0, 0)),
        scratch_shapes=[
            pltpu.VMEM((SLOTS, KVH * HD), bf16),
            pltpu.VMEM((SLOTS, KVH * HD), bf16),
            pltpu.VMEM((SLOTS, 1), f32),
            pltpu.VMEM((SLOTS, 1), f32),
        ],
        compiler_params=pltpu.CompilerParams(vmem_limit_bytes=32 << 20),
        cost_estimate=pl.CostEstimate(
            flops=1_200_000_000, bytes_accessed=21_000_000, transcendentals=0
        ),
        name="project",
    )(sc, tok, wk, wv, embed)


def norm_kernel(owner_ref, recv_ref, embed_ref, scale_ref, out_ref):
    tail = recv_ref[0, :, FS:].astype(f32)
    lane = lax.broadcasted_iota(jnp.int32, (SLOTS, 128), 1)
    inv = jnp.sum(jnp.where(lane < 3, tail, 0.0), 1, keepdims=True)
    cross = jnp.sum(jnp.where(lane >= 3, tail, 0.0), 1, keepdims=True)
    scaled = scale_ref[...] * recv_ref[0, :, :FS].astype(f32)
    rows = embed_ref[0].astype(f32)
    out_ref[0] = inv * scaled - rows * (inv * inv * inv * cross)


def norm_grads(owner, recv, embed, scale):
    return pl.pallas_call(
        norm_kernel,
        out_shape=jax.ShapeDtypeStruct((NDP, SLOTS, FS), f32),
        grid_spec=pltpu.PrefetchScalarGridSpec(
            num_scalar_prefetch=1,
            grid=(NDP,),
            in_specs=[
                pl.BlockSpec((1, SLOTS, FS + 128), lambda b, owner: (b, 0, 0)),
                pl.BlockSpec((1, SLOTS, FS), lambda b, owner: (owner[b], 0, 0)),
                pl.BlockSpec((1, FS), lambda b, owner: (0, 0)),
            ],
            out_specs=pl.BlockSpec((1, SLOTS, FS), lambda b, owner: (owner[b], 0, 0)),
        ),
        name="norm_grads",
    )(owner, recv, embed, scale)


def exchange(x, axes):
    return lax.all_to_all(x, axes, split_axis=0, concat_axis=0, tiled=True)


def swap(x, axis):
    return lax.ppermute(x, axis, [(0, 1), (1, 0)])


def local(
    query_states,
    key_states,
    value_states,
    out_grads,
    image_counts,
    prefix_lengths,
    encoder_owner,
    key_weight,
    value_weight,
    norm_scale,
    image_embed,
):
    ctx = ("y", "zh", "zl", "core")
    scale = norm_scale.reshape(1, FS)
    sc = jnp.stack([prefix_lengths[0], lax.axis_index("zh"), lax.axis_index("core")]).astype(
        jnp.int32
    )
    tok_sc = jnp.stack([image_counts[0], lax.axis_index(ctx)]).astype(jnp.int32)

    kv0 = exchange(pack_heads(key_states[0], value_states[0], "pack_kv"), ("y", "zl"))
    kv1 = swap(kv0, "core")
    kv2 = swap(kv0, "zh")
    kv3 = swap(kv2, "core")
    qd = exchange(pack_heads(query_states[0], out_grads[0], "pack_qd"), ("y", "zl"))
    embed_full = exchange(pack_embed(encoder_owner, image_embed, scale), "dp")

    dq, own, core_part, far, farcore, tok = attention(sc, qd, kv0, kv1, kv2, kv3)

    tok_in = exchange(tok, ctx)
    far_sum = pair_sum(far, swap(farcore, "core"))
    dkv = last_sum(own, swap(core_part, "core"), swap(far_sum, "zh"))
    payload = project(tok_sc, tok_in, key_weight, value_weight, embed_full)
    recv = exchange(payload, "dp")
    dq_in = exchange(dq, ("y", "zl"))
    dkv_in = exchange(dkv, ("y", "zl"))
    image_grads = norm_grads(encoder_owner, recv, image_embed, scale)
    query_grads, key_grads, value_grads = unpack(dq_in, dkv_in)
    return (query_grads[None], key_grads[None], value_grads[None], image_grads)


def solution(mesh):
    ctx = ("y", "zh", "zl", "core")
    split = Mesh(mesh.devices.reshape(4, 4, 2, 2, 2), ("dp",) + ctx)
    rows = P("dp", ctx, None)
    image = P(None, ctx, "dp")
    in_specs = (rows, rows, rows, rows, P("dp"), P("dp"), P(), P(), P(), P("dp"), image)
    out_specs = (rows, rows, rows, image)
    return jax.shard_map(local, mesh=split, in_specs=in_specs, out_specs=out_specs, check_vma=False)
```

```python
import functools
import math

import jax
import jax.numpy as jnp
from jax import lax
from jax.experimental import pallas as pl
from jax.experimental.pallas import tpu as pltpu
from jax.sharding import Mesh, PartitionSpec as P

D = 4608
HD = 128
KVH = 8
TOK = 128
SLOTS = 64
NDP = 4
FS = D // NDP
SEG = 512
NSEG = 8

score_scale = 144.0 ** (-0.5)
soft_cap = 50.0
norm_eps = 1e-06
tanh_scale = score_scale / soft_cap
exp2_scale = soft_cap * math.log2(math.e)

f32 = jnp.float32
bf16 = jnp.bfloat16
VM = pl.BlockSpec(memory_space=pltpu.VMEM)
ANY = pl.BlockSpec(memory_space=pl.ANY)
SM = pl.BlockSpec(memory_space=pltpu.SMEM)
NT = (((1,), (1,)), ((), ()))
NN = (((1,), (0,)), ((), ()))


def mm(a, b, dims=NN):
    return lax.dot_general(a, b, dims, preferred_element_type=f32)


def split3(x):
    hi = x.astype(bf16)
    rest = x - hi.astype(f32)
    mid = rest.astype(bf16)
    lo = (rest - mid.astype(f32)).astype(bf16)
    return hi, mid, lo


def params(mib):
    return pltpu.CompilerParams(vmem_limit_bytes=mib << 20)


def cost(us, flops=0):
    return pl.CostEstimate(flops=flops, bytes_accessed=int(us * 3_000_000), transcendentals=0)


def pack_kernel(width, a_ref, b_ref, out_ref):
    for h in range(KVH):
        out_ref[h, :, :width] = a_ref[:, h * width : (h + 1) * width]
        out_ref[h, :, width:] = b_ref[:, h * width : (h + 1) * width]


def pack_heads(a, b, name):
    width = a.shape[1] // KVH
    return pl.pallas_call(
        functools.partial(pack_kernel, width),
        out_shape=jax.ShapeDtypeStruct((KVH, TOK, 2 * width), bf16),
        in_specs=[VM, VM],
        out_specs=VM,
        compiler_params=params(60),
        cost_estimate=cost(2),
        name=name,
    )(a, b)


def embed_pack_kernel(sc_ref, embed_ref, scale_ref, *out_refs):
    row = lax.broadcasted_iota(jnp.int32, (16, FS), 0)
    hi, mid, lo = split3(scale_ref[...].reshape(1, FS))
    parts = jnp.where(row == 0, hi.astype(f32), jnp.where(row == 1, mid.astype(f32), 0.0))
    parts = jnp.where(row == 2, lo.astype(f32), parts).astype(bf16)
    for n in range(NDP):
        out_refs[n][:SLOTS, :] = embed_ref[sc_ref[n]]
        out_refs[n][SLOTS:, :] = parts


def pack_embed(sc, embed, scale):
    one = jax.ShapeDtypeStruct((SLOTS + 16, FS), bf16)
    return pl.pallas_call(
        embed_pack_kernel,
        out_shape=(one,) * NDP,
        in_specs=[SM, VM, VM],
        out_specs=(VM,) * NDP,
        compiler_params=params(8),
        cost_estimate=cost(3),
        name="pack_embed",
    )(sc, embed, scale)


def attention_kernel(
    sc_ref,
    qd_ref,
    kv0_ref,
    kv1_ref,
    kv2_ref,
    kv3_ref,
    dq_ref,
    own_ref,
    core_ref,
    far_ref,
    farcore_ref,
    tok_ref,
    k_s,
    v_s,
    kt_s,
    q_s,
    do_s,
    e_s,
    w_s,
    p_s,
    dk_s,
    dv_s,
    tot,
    mom,
    dqt,
    perm,
    dot_s,
):
    prefix, zh, core = sc_ref[0], sc_ref[1], sc_ref[2]
    eye = (
        lax.broadcasted_iota(jnp.int32, (HD, HD), 0) == lax.broadcasted_iota(jnp.int32, (HD, HD), 1)
    ).astype(bf16)
    for seg in range(NSEG):
        near, away = ((kv0_ref, kv1_ref), (kv2_ref, kv3_ref))[seg // 4]
        y = seg % 4
        whole = jnp.concatenate([near[2 * y], near[2 * y + 1], away[2 * y], away[2 * y + 1]], 0)
        k_s[seg] = whole[:, :HD]
        v_s[seg] = whole[:, HD:]
        kt_s[seg] = mm(eye, whole[:, :HD], NT).astype(bf16)
    dk_s[...] = jnp.zeros_like(dk_s)
    dv_s[...] = jnp.zeros_like(dv_s)

    def key_start(j):
        far = j // 4
        return (j % 4) * 1024 + (zh + far - 2 * zh * far) * SEG

    def hidden(key0, row0):
        s = lax.broadcasted_iota(jnp.int32, (SEG, SEG), 0)
        piece = s // TOK
        other = piece // 2
        key = key0 + (piece % 2) * 256 + (core + other - 2 * core * other) * TOK + s % TOK
        lane = lax.broadcasted_iota(jnp.int32, (1, SEG), 1)
        row = row0 + ((lane // TOK) % 2) * 256 + lane % TOK
        return key >= jnp.maximum(row + 1, prefix)

    def row_body(i, _):
        row0 = i * 1024 + zh * SEG + core * TOK
        limit = jnp.maximum(prefix, row0 + 384)
        full = jnp.maximum(prefix, row0 + 1)
        for head in range(2):
            for z in range(2):
                at = pl.ds((head * 2 + z) * TOK, TOK)
                q_s[at, :] = qd_ref[2 * i + z, :, head * HD : (head + 1) * HD]
                do_s[at, :] = qd_ref[2 * i + z, :, (2 + head) * HD : (3 + head) * HD]
        tot[...] = jnp.zeros_like(tot)
        mom[...] = jnp.zeros_like(mom)
        dqt[...] = jnp.zeros_like(dqt)

        def scores(y, masked):
            pair = (y, y + 4)
            ts = [jnp.tanh(mm(k_s[j], q_s[...], NT) * tanh_scale) for j in pair]
            dps = [mm(v_s[j], do_s[...], NT) for j in pair]
            total, moment = tot[...], mom[...]
            for j, t, dp in zip(pair, ts, dps):
                e = jnp.exp2(t * exp2_scale)
                if masked:
                    e = jnp.where(hidden(key_start(j), row0), 0.0, e)
                total += jnp.sum(e, 0, keepdims=True)
                moment += jnp.sum(e * dp, 0, keepdims=True)
                e_s[j] = e.astype(bf16)
                w_s[j] = e * (1.0 - t * t)
                p_s[j] = dp
            tot[...], mom[...] = total, moment

        def first(y, _):
            @pl.when(y * 1024 + 1024 <= full)
            def _():
                scores(y, False)

            @pl.when((y * 1024 + 1024 > full) & (y * 1024 < limit))
            def _():
                scores(y, True)

            return 0

        lax.fori_loop(0, 4, first, 0)
        inv = 1.0 / tot[...]
        delta = mom[...] * inv
        dot_s[...] = (mm(eye, do_s[...], NT) * inv).astype(bf16)

        def second(y, _):
            @pl.when(y * 1024 < limit)
            def _():
                grad = dqt[...]
                for j in (y, y + 4):
                    ds = (w_s[j] * inv * (p_s[j] - delta)).astype(bf16)
                    dv_s[j] += mm(e_s[j], dot_s[...], NT)
                    dk_s[j] += mm(ds, q_s[...])
                    grad += mm(kt_s[j], ds)
                dqt[...] = grad

            return 0

        lax.fori_loop(0, 4, second, 0)
        dq = (dqt[...] * score_scale).T.astype(bf16)
        for head in range(2):
            for z in range(2):
                at = (head * 2 + z) * TOK
                dq_ref[2 * i + z, :, head * HD : (head + 1) * HD] = dq[at : at + TOK]
        return 0

    lax.fori_loop(0, 4, row_body, 0)

    out = lax.broadcasted_iota(jnp.int32, (SEG, SEG), 0)
    src = lax.broadcasted_iota(jnp.int32, (SEG, SEG), 1)
    slot = out % 16
    c_of = (slot // 4) % 2
    want = (
        (c_of + core - 2 * c_of * core) * 256 + (slot // 8) * TOK + (slot % 4) * 32 + out // 16
    )
    perm[...] = (want == src).astype(bf16)
    for seg in range(NSEG):
        near, away = ((own_ref, core_ref), (far_ref, farcore_ref))[seg // 4]
        y = seg % 4
        terms = jnp.concatenate([dk_s[seg] * score_scale, dv_s[seg]], 1)
        near[2 * y] = terms[:TOK].astype(near.dtype)
        near[2 * y + 1] = terms[TOK : 2 * TOK].astype(near.dtype)
        away[2 * y] = terms[2 * TOK : 3 * TOK].astype(away.dtype)
        away[2 * y + 1] = terms[3 * TOK :].astype(away.dtype)
        if y < 2:
            moved = mm(perm[...], terms.astype(bf16)).astype(bf16).reshape(32, 16, 2 * HD)
            z_at = zh if seg < 4 else 1 - zh
            tok_ref[:, pl.ds(pl.multiple_of((2 * y + z_at) * 16, 16), 16), :] = moved


def attention(sc, qd, kv0, kv1, kv2, kv3):
    part = (KVH, TOK, 2 * HD)
    return pl.pallas_call(
        attention_kernel,
        out_shape=(
            jax.ShapeDtypeStruct(part, bf16),
            jax.ShapeDtypeStruct(part, f32),
            jax.ShapeDtypeStruct(part, bf16),
            jax.ShapeDtypeStruct(part, bf16),
            jax.ShapeDtypeStruct(part, bf16),
            jax.ShapeDtypeStruct((32, SLOTS, 2 * HD), bf16),
        ),
        in_specs=[SM] + [VM] * 5,
        out_specs=(VM,) * 6,
        scratch_shapes=[
            pltpu.VMEM((NSEG, SEG, HD), bf16),
            pltpu.VMEM((NSEG, SEG, HD), bf16),
            pltpu.VMEM((NSEG, HD, SEG), bf16),
            pltpu.VMEM((SEG, HD), bf16),
            pltpu.VMEM((SEG, HD), bf16),
            pltpu.VMEM((NSEG, SEG, SEG), bf16),
            pltpu.VMEM((NSEG, SEG, SEG), f32),
            pltpu.VMEM((NSEG, SEG, SEG), f32),
            pltpu.VMEM((NSEG, SEG, HD), f32),
            pltpu.VMEM((NSEG, SEG, HD), f32),
            pltpu.VMEM((1, SEG), f32),
            pltpu.VMEM((1, SEG), f32),
            pltpu.VMEM((HD, SEG), f32),
            pltpu.VMEM((SEG, SEG), bf16),
            pltpu.VMEM((HD, SEG), bf16),
        ],
        compiler_params=params(60),
        cost_estimate=cost(36),
        name="attention",
    )(sc, qd, kv0, kv1, kv2, kv3)


def pair_sum_kernel(a_ref, b_ref, out_ref):
    out_ref[...] = (a_ref[...].astype(f32) + b_ref[...].astype(f32)).astype(bf16)


def pair_sum(a, b):
    return pl.pallas_call(
        pair_sum_kernel,
        out_shape=jax.ShapeDtypeStruct(a.shape, bf16),
        in_specs=[VM, VM],
        out_specs=VM,
        compiler_params=params(8),
        cost_estimate=cost(2),
        name="pair_sum",
    )(a, b)


def last_sum_kernel(dq_ref, a_ref, b_ref, c_ref, _, out_ref):
    out_ref[:, :, : 2 * HD] = dq_ref[...]
    total = a_ref[...] + b_ref[...].astype(f32) + c_ref[...].astype(f32)
    out_ref[:, :, 2 * HD :] = total.astype(bf16)


def last_sum(dq, a, b, c, after):
    return pl.pallas_call(
        last_sum_kernel,
        out_shape=jax.ShapeDtypeStruct((KVH, TOK, 4 * HD), bf16),
        in_specs=[VM] * 4 + [ANY],
        out_specs=VM,
        compiler_params=params(8),
        cost_estimate=cost(3),
        name="last_sum",
    )(dq, a, b, c, after)


def unpack_kernel(in_ref, q_ref, k_ref, v_ref):
    for h in range(KVH):
        q_ref[:, h * 2 * HD : (h + 1) * 2 * HD] = in_ref[h, :, : 2 * HD]
        k_ref[:, h * HD : (h + 1) * HD] = in_ref[h, :, 2 * HD : 3 * HD]
        v_ref[:, h * HD : (h + 1) * HD] = in_ref[h, :, 3 * HD :]


def unpack(grads):
    return pl.pallas_call(
        unpack_kernel,
        out_shape=(
            jax.ShapeDtypeStruct((TOK, 2 * KVH * HD), bf16),
            jax.ShapeDtypeStruct((TOK, KVH * HD), bf16),
            jax.ShapeDtypeStruct((TOK, KVH * HD), bf16),
        ),
        in_specs=[VM],
        out_specs=(VM, VM, VM),
        compiler_params=params(8),
        cost_estimate=cost(2),
        name="unpack",
    )(grads)


def project_kernel(
    sc_ref, tok_ref, wk_ref, wv_ref, e0, e1, e2, e3, o0, o1, o2, o3, wk_s, wv_s, sems
):
    copies = []
    for n in range(NDP):
        at = pl.ds(pl.multiple_of(lax.rem(sc_ref[5] + NDP - n, NDP) * FS, FS), FS)
        pair = (
            pltpu.make_async_copy(wk_ref.at[at], wk_s.at[n], sems.at[n, 0]),
            pltpu.make_async_copy(wv_ref.at[at], wv_s.at[n], sems.at[n, 1]),
        )
        for copy in pair:
            copy.start()
        copies.append(pair)
    xk, xv = [], []
    for h in range(KVH):
        base = (h // 2) * 8 + (h % 2) * 2
        total = tok_ref[base].astype(f32) + tok_ref[base + 1].astype(f32)
        total = total + tok_ref[base + 4].astype(f32) + tok_ref[base + 5].astype(f32)
        total = total.astype(bf16)
        xk.append(total[:, :HD])
        xv.append(total[:, HD:])
    xk, xv = jnp.concatenate(xk, 1), jnp.concatenate(xv, 1)
    token = lax.broadcasted_iota(jnp.int32, (SLOTS, FS), 0) * 32 + sc_ref[4]
    visible = token < sc_ref[3]
    sq = jnp.zeros((SLOTS, 1), f32)
    cross = jnp.zeros((SLOTS, 1), f32)
    outs = (o0, o1, o2, o3)
    for n, embed_ref in enumerate((e0, e1, e2, e3)):
        rows = embed_ref[:SLOTS, :].astype(f32)
        tail = embed_ref[SLOTS:, :].astype(f32)
        scale = tail[0:1] + tail[1:2] + tail[2:3]
        sq += jnp.sum(rows * rows, 1, keepdims=True)
        for copy in copies[n]:
            copy.wait()
        projected = mm(xk, wk_s[n], NT) + mm(xv, wv_s[n], NT)
        grad = jnp.where(visible, projected, 0.0).astype(bf16)
        outs[n][:, :FS] = grad
        cross += jnp.sum(rows * (scale * grad.astype(f32)), 1, keepdims=True)
    lane = lax.broadcasted_iota(jnp.int32, (SLOTS, 128), 1)
    parts = split3(lax.rsqrt(sq / D + norm_eps)) + split3(cross / D)
    tail = jnp.zeros((SLOTS, 128), f32)
    for n, part in enumerate(parts):
        tail = jnp.where(lane == n, part.astype(f32), tail)
    for n in range(NDP):
        outs[n][:, FS:] = tail.astype(bf16)


def project(sc, tok, wk, wv, embeds):
    one = jax.ShapeDtypeStruct((SLOTS, FS + 128), bf16)
    return pl.pallas_call(
        project_kernel,
        out_shape=(one,) * NDP,
        in_specs=[SM, VM, ANY, ANY] + [VM] * 4,
        out_specs=(VM,) * NDP,
        scratch_shapes=[
            pltpu.VMEM((NDP, FS, KVH * HD), bf16),
            pltpu.VMEM((NDP, FS, KVH * HD), bf16),
            pltpu.SemaphoreType.DMA((NDP, 2)),
        ],
        compiler_params=params(60),
        cost_estimate=cost(10),
        name="project",
    )(sc, tok, wk, wv, *embeds)


def norm_kernel(sc_ref, r0, r1, r2, r3, embed_ref, scale_ref, out_ref):
    lane = lax.broadcasted_iota(jnp.int32, (SLOTS, 128), 1)
    scale = scale_ref[...].reshape(1, FS)
    for n, recv_ref in enumerate((r0, r1, r2, r3)):
        row = sc_ref[n]
        tail = recv_ref[:, FS:].astype(f32)
        inv = jnp.sum(jnp.where(lane < 3, tail, 0.0), 1, keepdims=True)
        cross = jnp.sum(jnp.where(lane >= 3, tail, 0.0), 1, keepdims=True)
        scaled = scale * recv_ref[:, :FS].astype(f32)
        rows = embed_ref[row].astype(f32)
        out_ref[row] = inv * scaled - rows * (inv * inv * inv * cross)


def norm_grads(sc, recvs, embed, scale):
    return pl.pallas_call(
        norm_kernel,
        out_shape=jax.ShapeDtypeStruct((NDP, SLOTS, FS), f32),
        in_specs=[SM] + [VM] * 6,
        out_specs=VM,
        compiler_params=params(8),
        cost_estimate=cost(3),
        name="norm_grads",
    )(sc, *recvs, embed, scale)


def exchange(x, axes):
    return lax.all_to_all(x, axes, split_axis=0, concat_axis=0, tiled=True)


def shift(x, by):
    return lax.ppermute(x, "dp", [(i, (i + by) % NDP) for i in range(NDP)])


def swap(x, axis):
    return lax.ppermute(x, axis, [(0, 1), (1, 0)])


def local(
    query_states,
    key_states,
    value_states,
    out_grads,
    image_counts,
    prefix_lengths,
    encoder_owner,
    key_weight,
    value_weight,
    norm_scale,
    image_embed,
):
    ctx = ("y", "zh", "zl", "core")
    dp = lax.axis_index("dp")
    sc = jnp.stack(
        [
            prefix_lengths[0],
            lax.axis_index("zh"),
            lax.axis_index("core"),
            image_counts[0],
            lax.axis_index(ctx),
            dp,
        ]
    ).astype(jnp.int32)
    owner = lax.dynamic_slice(jnp.concatenate([encoder_owner, encoder_owner]), (dp,), (NDP,))

    kv0 = exchange(pack_heads(key_states[0], value_states[0], "pack_kv"), ("y", "zl"))
    kv1 = swap(kv0, "core")
    kv2 = swap(kv0, "zh")
    kv3 = swap(kv2, "core")
    qd = exchange(pack_heads(query_states[0], out_grads[0], "pack_qd"), ("y", "zl"))

    dq, own, core_part, far, farcore, tok = attention(sc, qd, kv0, kv1, kv2, kv3)

    packed = pack_embed(owner, image_embed, norm_scale)
    embeds = [packed[0]] + [shift(packed[n], n) for n in range(1, NDP)]
    tok_in = exchange(tok, ctx)
    far_sum = pair_sum(far, swap(farcore, "core"))
    payload = project(sc, tok_in, key_weight, value_weight, embeds)
    grads = last_sum(dq, own, swap(core_part, "core"), swap(far_sum, "zh"), payload[0])
    recvs = [payload[0]] + [shift(payload[n], -n) for n in range(1, NDP)]
    image_grads = norm_grads(owner, recvs, image_embed, norm_scale)
    query_grads, key_grads, value_grads = unpack(exchange(grads, ("y", "zl")))
    return (query_grads[None], key_grads[None], value_grads[None], image_grads)


def solution(mesh):
    ctx = ("y", "zh", "zl", "core")
    split = Mesh(mesh.devices.reshape(4, 4, 2, 2, 2), ("dp",) + ctx)
    rows = P("dp", ctx, None)
    image = P(None, ctx, "dp")
    in_specs = (rows, rows, rows, rows, P("dp"), P("dp"), P(), P(), P(), P("dp"), image)
    out_specs = (rows, rows, rows, image)
    return jax.shard_map(local, mesh=split, in_specs=in_specs, out_specs=out_specs, check_vma=False)
```

```python
import functools
import math

import jax
import jax.numpy as jnp
from jax import lax
from jax.experimental import pallas as pl
from jax.experimental.pallas import tpu as pltpu
from jax.sharding import Mesh, PartitionSpec as P

D = 4608
HD = 128
KVH = 8
TOK = 128
SLOTS = 64
NDP = 4
FS = D // NDP
SEG = 512
NSEG = 8

score_scale = 144.0 ** (-0.5)
soft_cap = 50.0
norm_eps = 1e-06
tanh_scale = score_scale / soft_cap
exp2_scale = soft_cap * math.log2(math.e)

f32 = jnp.float32
bf16 = jnp.bfloat16
VM = pl.BlockSpec(memory_space=pltpu.VMEM)
ANY = pl.BlockSpec(memory_space=pl.ANY)
SM = pl.BlockSpec(memory_space=pltpu.SMEM)
NT = (((1,), (1,)), ((), ()))
NN = (((1,), (0,)), ((), ()))


def mm(a, b, dims=NN):
    return lax.dot_general(a, b, dims, preferred_element_type=f32)


def split3(x):
    hi = x.astype(bf16)
    rest = x - hi.astype(f32)
    mid = rest.astype(bf16)
    lo = (rest - mid.astype(f32)).astype(bf16)
    return hi, mid, lo


def params(mib):
    return pltpu.CompilerParams(vmem_limit_bytes=mib << 20)


def cost(us, flops=0):
    return pl.CostEstimate(flops=flops, bytes_accessed=int(us * 3_000_000), transcendentals=0)


def pack_kernel(width, sc_ref, a_ref, b_ref, out_ref):
    for h in range(KVH):
        at = (h // 2) * 2 + (h % 2 + sc_ref[1] - 2 * (h % 2) * sc_ref[1])
        out_ref[at, :, :width] = a_ref[:, h * width : (h + 1) * width]
        out_ref[at, :, width:] = b_ref[:, h * width : (h + 1) * width]


def pack_heads(sc, a, b, name):
    width = a.shape[1] // KVH
    return pl.pallas_call(
        functools.partial(pack_kernel, width),
        out_shape=jax.ShapeDtypeStruct((KVH, TOK, 2 * width), bf16),
        in_specs=[SM, VM, VM],
        out_specs=VM,
        compiler_params=params(60),
        cost_estimate=cost(2),
        name=name,
    )(sc, a, b)


def mixed_kernel(
    sc_ref, owner_ref, embed_ref, scale_ref, wk_ref, wv_ref, mark_ref, u0, u1, u2, u3, wk_s, wv_s, sems
):
    at = pl.ds(pl.multiple_of(sc_ref[5] * FS, FS), FS)
    copies = (
        pltpu.make_async_copy(wk_ref.at[at], wk_s, sems.at[0]),
        pltpu.make_async_copy(wv_ref.at[at], wv_s, sems.at[1]),
    )
    for copy in copies:
        copy.start()
    mark_ref[...] = jnp.zeros_like(mark_ref)
    lane = lax.broadcasted_iota(jnp.int32, (SLOTS, 128), 1)
    scale = scale_ref[...].reshape(1, FS)
    outs = (u0, u1, u2, u3)
    scaled = []
    for n in range(NDP):
        rows = embed_ref[owner_ref[n]].astype(f32)
        tail = jnp.zeros((SLOTS, 128), f32)
        for k, part in enumerate(split3(jnp.sum(rows * rows, 1, keepdims=True))):
            tail = jnp.where(lane == k, part.astype(f32), tail)
        outs[n][:, 2 * KVH * HD :] = tail.astype(bf16)
        scaled.append((rows * scale).astype(bf16))
    scaled = jnp.concatenate(scaled, 0)
    for half, (copy, w_s) in enumerate(zip(copies, (wk_s, wv_s))):
        copy.wait()
        mixed = mm(scaled, w_s[...]).astype(bf16)
        for n in range(NDP):
            outs[n][:, half * KVH * HD : (half + 1) * KVH * HD] = mixed[
                n * SLOTS : (n + 1) * SLOTS
            ]


def mix(sc, owner, embed, scale, wk, wv):
    one = jax.ShapeDtypeStruct((SLOTS, 2 * KVH * HD + 128), bf16)
    return pl.pallas_call(
        mixed_kernel,
        out_shape=(jax.ShapeDtypeStruct((8, 128), f32),) + (one,) * NDP,
        in_specs=[SM, SM, VM, VM, ANY, ANY],
        out_specs=(VM,) * (NDP + 1),
        scratch_shapes=[
            pltpu.VMEM((FS, KVH * HD), bf16),
            pltpu.VMEM((FS, KVH * HD), bf16),
            pltpu.SemaphoreType.DMA((2,)),
        ],
        compiler_params=params(60),
        cost_estimate=cost(5),
        name="mix",
    )(sc, owner, embed, scale, wk, wv)


def join(x, *after):
    return pl.pallas_call(
        lambda *refs: None,
        out_shape=jax.ShapeDtypeStruct(x.shape, x.dtype),
        in_specs=[ANY] * (1 + len(after)),
        out_specs=ANY,
        input_output_aliases={0: 0},
        compiler_params=params(2),
        cost_estimate=cost(1),
        name="join",
    )(x, *after)


def attention_kernel(
    sc_ref,
    qd_ref,
    kv0_ref,
    kv1_ref,
    kv2_ref,
    kv3_ref,
    dq_ref,
    own_ref,
    core_ref,
    far_ref,
    farcore_ref,
    tok_ref,
    k_s,
    v_s,
    kt_s,
    q_s,
    do_s,
    e_s,
    w_s,
    p_s,
    dk_s,
    dv_s,
    tot,
    mom,
    dqt,
    perm,
    dot_s,
):
    prefix, zh, core = sc_ref[0], sc_ref[1], sc_ref[2]
    eye = (
        lax.broadcasted_iota(jnp.int32, (HD, HD), 0) == lax.broadcasted_iota(jnp.int32, (HD, HD), 1)
    ).astype(bf16)
    for seg in range(NSEG):
        near, away = ((kv0_ref, kv1_ref), (kv2_ref, kv3_ref))[seg // 4]
        y = seg % 4
        whole = jnp.concatenate([near[2 * y], near[2 * y + 1], away[2 * y], away[2 * y + 1]], 0)
        k_s[seg] = whole[:, :HD]
        v_s[seg] = whole[:, HD:]
        kt_s[seg] = mm(eye, whole[:, :HD], NT).astype(bf16)
    dk_s[...] = jnp.zeros_like(dk_s)
    dv_s[...] = jnp.zeros_like(dv_s)

    def key_start(j):
        far = j // 4
        return (j % 4) * 1024 + (zh + far - 2 * zh * far) * SEG

    def hidden(key0, row0):
        s = lax.broadcasted_iota(jnp.int32, (SEG, SEG), 0)
        piece = s // TOK
        other = piece // 2
        key = key0 + (piece % 2) * 256 + (core + other - 2 * core * other) * TOK + s % TOK
        lane = lax.broadcasted_iota(jnp.int32, (1, SEG), 1)
        row = row0 + ((lane // TOK) % 2) * 256 + lane % TOK
        return key >= jnp.maximum(row + 1, prefix)

    def row_body(i, _):
        row0 = i * 1024 + zh * SEG + core * TOK
        limit = jnp.maximum(prefix, row0 + 384)
        full = jnp.maximum(prefix, row0 + 1)
        for head in range(2):
            for z in range(2):
                at = pl.ds((head * 2 + z) * TOK, TOK)
                q_s[at, :] = qd_ref[2 * i + z, :, head * HD : (head + 1) * HD]
                do_s[at, :] = qd_ref[2 * i + z, :, (2 + head) * HD : (3 + head) * HD]
        tot[...] = jnp.zeros_like(tot)
        mom[...] = jnp.zeros_like(mom)
        dqt[...] = jnp.zeros_like(dqt)

        def scores(y, masked):
            pair = (y, y + 4)
            ts = [jnp.tanh(mm(k_s[j], q_s[...], NT) * tanh_scale) for j in pair]
            dps = [mm(v_s[j], do_s[...], NT) for j in pair]
            total, moment = tot[...], mom[...]
            for j, t, dp in zip(pair, ts, dps):
                e = jnp.exp2(t * exp2_scale)
                if masked:
                    e = jnp.where(hidden(key_start(j), row0), 0.0, e)
                total += jnp.sum(e, 0, keepdims=True)
                moment += jnp.sum(e * dp, 0, keepdims=True)
                e_s[j] = e.astype(bf16)
                w_s[j] = e * (1.0 - t * t)
                p_s[j] = dp
            tot[...], mom[...] = total, moment

        def first(y, _):
            @pl.when(y * 1024 + 1024 <= full)
            def _():
                scores(y, False)

            @pl.when((y * 1024 + 1024 > full) & (y * 1024 < limit))
            def _():
                scores(y, True)

            return 0

        lax.fori_loop(0, 4, first, 0)
        inv = 1.0 / tot[...]
        delta = mom[...] * inv
        dot_s[...] = (mm(eye, do_s[...], NT) * inv).astype(bf16)

        def second(y, _):
            @pl.when(y * 1024 < limit)
            def _():
                grad = dqt[...]
                for j in (y, y + 4):
                    ds = (w_s[j] * inv * (p_s[j] - delta)).astype(bf16)
                    dv_s[j] += mm(e_s[j], dot_s[...], NT)
                    dk_s[j] += mm(ds, q_s[...])
                    grad += mm(kt_s[j], ds)
                dqt[...] = grad

            return 0

        lax.fori_loop(0, 4, second, 0)
        dq = (dqt[...] * score_scale).T.astype(bf16)
        for head in range(2):
            for z in range(2):
                at = (head * 2 + z) * TOK
                dq_ref[2 * i + z, :, head * HD : (head + 1) * HD] = dq[at : at + TOK]
        return 0

    lax.fori_loop(0, 4, row_body, 0)

    out = lax.broadcasted_iota(jnp.int32, (SEG, SEG), 0)
    src = lax.broadcasted_iota(jnp.int32, (SEG, SEG), 1)
    slot = out % 16
    c_of = (slot // 4) % 2
    want = (
        (c_of + core - 2 * c_of * core) * 256 + (slot // 8) * TOK + (slot % 4) * 32 + out // 16
    )
    perm[...] = (want == src).astype(bf16)
    for seg in range(NSEG):
        near, away = ((own_ref, core_ref), (far_ref, farcore_ref))[seg // 4]
        y = seg % 4
        terms = jnp.concatenate([dk_s[seg] * score_scale, dv_s[seg]], 1)
        near[2 * y] = terms[:TOK].astype(near.dtype)
        near[2 * y + 1] = terms[TOK : 2 * TOK].astype(near.dtype)
        away[2 * y] = terms[2 * TOK : 3 * TOK].astype(away.dtype)
        away[2 * y + 1] = terms[3 * TOK :].astype(away.dtype)
        if y < 2:
            moved = mm(perm[...], terms.astype(bf16)).astype(bf16).reshape(32, 16, 2 * HD)
            z_at = zh if seg < 4 else 1 - zh
            tok_ref[:, pl.ds(pl.multiple_of((2 * y + z_at) * 16, 16), 16), :] = moved


def attention(sc, qd, kv0, kv1, kv2, kv3):
    part = (KVH, TOK, 2 * HD)
    return pl.pallas_call(
        attention_kernel,
        out_shape=(
            jax.ShapeDtypeStruct(part, bf16),
            jax.ShapeDtypeStruct(part, f32),
            jax.ShapeDtypeStruct(part, bf16),
            jax.ShapeDtypeStruct(part, bf16),
            jax.ShapeDtypeStruct(part, bf16),
            jax.ShapeDtypeStruct((32, SLOTS, 2 * HD), bf16),
        ),
        in_specs=[SM] + [VM] * 5,
        out_specs=(VM,) * 6,
        scratch_shapes=[
            pltpu.VMEM((NSEG, SEG, HD), bf16),
            pltpu.VMEM((NSEG, SEG, HD), bf16),
            pltpu.VMEM((NSEG, HD, SEG), bf16),
            pltpu.VMEM((SEG, HD), bf16),
            pltpu.VMEM((SEG, HD), bf16),
            pltpu.VMEM((NSEG, SEG, SEG), bf16),
            pltpu.VMEM((NSEG, SEG, SEG), f32),
            pltpu.VMEM((NSEG, SEG, SEG), f32),
            pltpu.VMEM((NSEG, SEG, HD), f32),
            pltpu.VMEM((NSEG, SEG, HD), f32),
            pltpu.VMEM((1, SEG), f32),
            pltpu.VMEM((1, SEG), f32),
            pltpu.VMEM((HD, SEG), f32),
            pltpu.VMEM((SEG, SEG), bf16),
            pltpu.VMEM((HD, SEG), bf16),
        ],
        compiler_params=params(60),
        cost_estimate=cost(36),
        name="attention",
    )(sc, qd, kv0, kv1, kv2, kv3)


def pair_sum_kernel(a_ref, b_ref, out_ref):
    out_ref[...] = (a_ref[...].astype(f32) + b_ref[...].astype(f32)).astype(bf16)


def pair_sum(a, b):
    return pl.pallas_call(
        pair_sum_kernel,
        out_shape=jax.ShapeDtypeStruct(a.shape, bf16),
        in_specs=[VM, VM],
        out_specs=VM,
        compiler_params=params(8),
        cost_estimate=cost(2, 30_000_000_000),
        name="pair_sum",
    )(a, b)


def last_sum_kernel(dq_ref, a_ref, b_ref, c_ref, _, out_ref):
    out_ref[:, :, : 2 * HD] = dq_ref[...]
    total = a_ref[...] + b_ref[...].astype(f32) + c_ref[...].astype(f32)
    out_ref[:, :, 2 * HD :] = total.astype(bf16)


def last_sum(dq, a, b, c, after):
    return pl.pallas_call(
        last_sum_kernel,
        out_shape=jax.ShapeDtypeStruct((KVH, TOK, 4 * HD), bf16),
        in_specs=[VM] * 4 + [ANY],
        out_specs=VM,
        compiler_params=params(8),
        cost_estimate=cost(3),
        name="last_sum",
    )(dq, a, b, c, after)


def unpack_kernel(sc_ref, in_ref, q_ref, k_ref, v_ref):
    for h in range(KVH):
        at = (h // 2) * 2 + (h % 2 + sc_ref[1] - 2 * (h % 2) * sc_ref[1])
        q_ref[:, h * 2 * HD : (h + 1) * 2 * HD] = in_ref[at, :, : 2 * HD]
        k_ref[:, h * HD : (h + 1) * HD] = in_ref[at, :, 2 * HD : 3 * HD]
        v_ref[:, h * HD : (h + 1) * HD] = in_ref[at, :, 3 * HD :]


def unpack(sc, grads):
    return pl.pallas_call(
        unpack_kernel,
        out_shape=(
            jax.ShapeDtypeStruct((TOK, 2 * KVH * HD), bf16),
            jax.ShapeDtypeStruct((TOK, KVH * HD), bf16),
            jax.ShapeDtypeStruct((TOK, KVH * HD), bf16),
        ),
        in_specs=[SM, VM],
        out_specs=(VM, VM, VM),
        compiler_params=params(8),
        cost_estimate=cost(2),
        name="unpack",
    )(sc, grads)


def token_kernel(sc_ref, tok_ref, u0, u1, u2, u3, out_ref):
    token = lax.broadcasted_iota(jnp.int32, (SLOTS, 2 * HD), 0) * 32 + sc_ref[4]
    visible = token < sc_ref[3]
    wide = KVH * HD
    cross = jnp.zeros((SLOTS, 1), f32)
    for h in range(KVH):
        base = (h // 2) * 8 + (h % 2) * 2
        away = (h // 2) * 8 + 4 + (1 - h % 2) * 2
        total = tok_ref[base].astype(f32) + tok_ref[base + 1].astype(f32)
        total = total + tok_ref[away].astype(f32) + tok_ref[away + 1].astype(f32)
        total = jnp.where(visible, total, 0.0).astype(bf16)
        for half in range(2):
            at = slice(half * wide + h * HD, half * wide + (h + 1) * HD)
            part = total[:, half * HD : (half + 1) * HD]
            out_ref[:, at] = part
            mixed = u0[:, at].astype(f32) + u1[:, at].astype(f32)
            mixed = mixed + u2[:, at].astype(f32) + u3[:, at].astype(f32)
            cross += jnp.sum(part.astype(f32) * mixed, 1, keepdims=True)
    lane = lax.broadcasted_iota(jnp.int32, (SLOTS, 128), 1)
    tail = u0[:, 2 * wide :].astype(f32) + u1[:, 2 * wide :].astype(f32)
    tail = tail + u2[:, 2 * wide :].astype(f32) + u3[:, 2 * wide :].astype(f32)
    sq = jnp.sum(tail, 1, keepdims=True)
    parts = split3(lax.rsqrt(sq / D + norm_eps)) + split3(cross / D)
    tail = jnp.zeros((SLOTS, 128), f32)
    for n, part in enumerate(parts):
        tail = jnp.where(lane == n, part.astype(f32), tail)
    out_ref[:, 2 * wide :] = tail.astype(bf16)


def token_rows(sc, tok, mixed):
    return pl.pallas_call(
        token_kernel,
        out_shape=jax.ShapeDtypeStruct((SLOTS, 2 * KVH * HD + 128), bf16),
        in_specs=[SM] + [VM] * 5,
        out_specs=VM,
        compiler_params=params(8),
        cost_estimate=cost(2),
        name="token_rows",
    )(sc, tok, *mixed)


def image_kernel(
    sc_ref, owner_ref, r0, r1, r2, r3, wk_ref, wv_ref, embed_ref, scale_ref, out_ref, wk_s, wv_s, sems
):
    at = pl.ds(pl.multiple_of(sc_ref[5] * FS, FS), FS)
    copies = (
        pltpu.make_async_copy(wk_ref.at[at], wk_s, sems.at[0]),
        pltpu.make_async_copy(wv_ref.at[at], wv_s, sems.at[1]),
    )
    for copy in copies:
        copy.start()
    wide = KVH * HD
    recvs = (r0, r1, r2, r3)
    xk = jnp.concatenate([r[:, :wide] for r in recvs], 0)
    xv = jnp.concatenate([r[:, wide : 2 * wide] for r in recvs], 0)
    copies[0].wait()
    projected = mm(xk, wk_s[...], NT)
    copies[1].wait()
    projected = projected + mm(xv, wv_s[...], NT)
    lane = lax.broadcasted_iota(jnp.int32, (SLOTS, 128), 1)
    scale = scale_ref[...].reshape(1, FS)
    for n, recv_ref in enumerate(recvs):
        row = owner_ref[n]
        tail = recv_ref[:, 2 * wide :].astype(f32)
        inv = jnp.sum(jnp.where(lane < 3, tail, 0.0), 1, keepdims=True)
        cross = jnp.sum(jnp.where(lane >= 3, tail, 0.0), 1, keepdims=True)
        grad = projected[n * SLOTS : (n + 1) * SLOTS].astype(bf16).astype(f32)
        rows = embed_ref[row].astype(f32)
        out_ref[row] = inv * (scale * grad) - rows * (inv * inv * inv * cross)


def image_out(sc, owner, recvs, wk, wv, embed, scale):
    return pl.pallas_call(
        image_kernel,
        out_shape=jax.ShapeDtypeStruct((NDP, SLOTS, FS), f32),
        in_specs=[SM, SM] + [VM] * 4 + [ANY, ANY, VM, VM],
        out_specs=VM,
        scratch_shapes=[
            pltpu.VMEM((FS, KVH * HD), bf16),
            pltpu.VMEM((FS, KVH * HD), bf16),
            pltpu.SemaphoreType.DMA((2,)),
        ],
        compiler_params=params(60),
        cost_estimate=cost(5, 60_000_000_000),
        name="image_out",
    )(sc, owner, *recvs, wk, wv, embed, scale)


def exchange(x, axes):
    return lax.all_to_all(x, axes, split_axis=0, concat_axis=0, tiled=True)


def shift(x, by):
    return lax.ppermute(x, "dp", [(i, (i + by) % NDP) for i in range(NDP)])


def mirror(x):
    return lax.ppermute(x, ("zh", "zl"), [(i, 3 - i) for i in range(4)])


def swap(x, axis):
    return lax.ppermute(x, axis, [(0, 1), (1, 0)])


def local(
    query_states,
    key_states,
    value_states,
    out_grads,
    image_counts,
    prefix_lengths,
    encoder_owner,
    key_weight,
    value_weight,
    norm_scale,
    image_embed,
):
    ctx = ("y", "zh", "zl", "core")
    dp = lax.axis_index("dp")
    sc = jnp.stack(
        [
            prefix_lengths[0],
            lax.axis_index("zh"),
            lax.axis_index("core"),
            image_counts[0],
            lax.axis_index(ctx),
            dp,
        ]
    ).astype(jnp.int32)
    owner = lax.dynamic_slice(jnp.concatenate([encoder_owner, encoder_owner]), (dp,), (NDP,))

    kv0 = exchange(pack_heads(sc, key_states[0], value_states[0], "pack_kv"), ("y", "zl"))
    qd_pack = pack_heads(sc, query_states[0], out_grads[0], "pack_qd")
    mark, *mixed = mix(sc, owner, image_embed, norm_scale, key_weight, value_weight)
    kv0 = join(kv0, mark, qd_pack)
    kv1 = swap(kv0, "core")
    mixed = [mixed[0]] + [shift(mixed[n], n) for n in range(1, NDP)]
    kv2 = join(mirror(kv0), mixed[1], mixed[3])
    kv3 = swap(kv2, "core")
    qd = exchange(qd_pack, ("y", "zl"))

    dq, own, core_part, far, farcore, tok = attention(sc, qd, kv0, kv1, kv2, kv3)

    tok_in = exchange(tok, ctx)
    far_sum = pair_sum(far, swap(farcore, "core"))
    rows = token_rows(sc, tok_in, mixed)
    grads = last_sum(dq, own, swap(core_part, "core"), mirror(far_sum), rows)
    recvs = [rows] + [shift(rows, -n) for n in range(1, NDP)]
    image_grads = image_out(
        sc, owner, recvs, key_weight, value_weight, image_embed, norm_scale
    )
    query_grads, key_grads, value_grads = unpack(sc, exchange(grads, ("y", "zl")))
    return (query_grads[None], key_grads[None], value_grads[None], image_grads)


def solution(mesh):
    ctx = ("y", "zh", "zl", "core")
    split = Mesh(mesh.devices.reshape(4, 4, 2, 2, 2), ("dp",) + ctx)
    rows = P("dp", ctx, None)
    image = P(None, ctx, "dp")
    in_specs = (rows, rows, rows, rows, P("dp"), P("dp"), P(), P(), P(), P("dp"), image)
    out_specs = (rows, rows, rows, image)
    return jax.shard_map(local, mesh=split, in_specs=in_specs, out_specs=out_specs, check_vma=False)
```

```python
import functools
import math

import jax
import jax.numpy as jnp
from jax import lax
from jax.experimental import pallas as pl
from jax.experimental.pallas import tpu as pltpu
from jax.sharding import Mesh, PartitionSpec as P

D = 4608
HD = 128
KVH = 8
TOK = 128
SLOTS = 64
NDP = 4
FS = D // NDP
SEG = 512
NSEG = 8

score_scale = 144.0 ** (-0.5)
soft_cap = 50.0
norm_eps = 1e-06
tanh_scale = score_scale / soft_cap
exp2_scale = soft_cap * math.log2(math.e)

f32 = jnp.float32
bf16 = jnp.bfloat16
VM = pl.BlockSpec(memory_space=pltpu.VMEM)
ANY = pl.BlockSpec(memory_space=pl.ANY)
SM = pl.BlockSpec(memory_space=pltpu.SMEM)
NT = (((1,), (1,)), ((), ()))
NN = (((1,), (0,)), ((), ()))


def mm(a, b, dims=NN):
    return lax.dot_general(a, b, dims, preferred_element_type=f32)


def split3(x):
    hi = x.astype(bf16)
    rest = x - hi.astype(f32)
    mid = rest.astype(bf16)
    lo = (rest - mid.astype(f32)).astype(bf16)
    return hi, mid, lo


def params(mib):
    return pltpu.CompilerParams(vmem_limit_bytes=mib << 20)


def cost(us, flops=0):
    return pl.CostEstimate(flops=flops, bytes_accessed=int(us * 3_000_000), transcendentals=0)


def pack_kernel(width, half_ref, a_ref, b_ref, out_ref):
    for h in range(KVH):
        at = (h // 2) * 2 + (h % 2 + half_ref[0] - 2 * (h % 2) * half_ref[0])
        out_ref[at, :, :width] = a_ref[:, h * width : (h + 1) * width]
        out_ref[at, :, width:] = b_ref[:, h * width : (h + 1) * width]


def pack_heads(half, a, b, name):
    width = a.shape[1] // KVH
    return pl.pallas_call(
        functools.partial(pack_kernel, width),
        out_shape=jax.ShapeDtypeStruct((KVH, TOK, 2 * width), bf16),
        in_specs=[SM, VM, VM],
        out_specs=VM,
        compiler_params=params(60),
        cost_estimate=cost(2),
        name=name,
    )(half, a, b)


def mixed_kernel(
    sc_ref, owner_ref, embed_ref, scale_ref, wk_ref, wv_ref, mark_ref, u0, u1, u2, u3, wk_s, wv_s, sems
):
    at = pl.ds(pl.multiple_of(sc_ref[5] * FS, FS), FS)
    copies = (
        pltpu.make_async_copy(wk_ref.at[at], wk_s, sems.at[0]),
        pltpu.make_async_copy(wv_ref.at[at], wv_s, sems.at[1]),
    )
    for copy in copies:
        copy.start()
    mark_ref[...] = jnp.zeros_like(mark_ref)
    lane = lax.broadcasted_iota(jnp.int32, (SLOTS, 128), 1)
    scale = scale_ref[...].reshape(1, FS)
    outs = (u0, u1, u2, u3)
    scaled = []
    for n in range(NDP):
        rows = embed_ref[owner_ref[n]].astype(f32)
        tail = jnp.zeros((SLOTS, 128), f32)
        for k, part in enumerate(split3(jnp.sum(rows * rows, 1, keepdims=True))):
            tail = jnp.where(lane == k, part.astype(f32), tail)
        outs[n][:, 2 * KVH * HD :] = tail.astype(bf16)
        scaled.append((rows * scale).astype(bf16))
    scaled = jnp.concatenate(scaled, 0)
    for half, (copy, w_s) in enumerate(zip(copies, (wk_s, wv_s))):
        copy.wait()
        mixed = mm(scaled, w_s[...]).astype(bf16)
        for n in range(NDP):
            outs[n][:, half * KVH * HD : (half + 1) * KVH * HD] = mixed[
                n * SLOTS : (n + 1) * SLOTS
            ]


def mix(sc, owner, embed, scale, wk, wv):
    one = jax.ShapeDtypeStruct((SLOTS, 2 * KVH * HD + 128), bf16)
    return pl.pallas_call(
        mixed_kernel,
        out_shape=(jax.ShapeDtypeStruct((8, 128), f32),) + (one,) * NDP,
        in_specs=[SM, SM, VM, VM, ANY, ANY],
        out_specs=(VM,) * (NDP + 1),
        scratch_shapes=[
            pltpu.VMEM((FS, KVH * HD), bf16),
            pltpu.VMEM((FS, KVH * HD), bf16),
            pltpu.SemaphoreType.DMA((2,)),
        ],
        compiler_params=params(60),
        cost_estimate=cost(5),
        name="mix",
    )(sc, owner, embed, scale, wk, wv)


def join(x, *after):
    return pl.pallas_call(
        lambda *refs: None,
        out_shape=jax.ShapeDtypeStruct(x.shape, x.dtype),
        in_specs=[ANY] * (1 + len(after)),
        out_specs=ANY,
        input_output_aliases={0: 0},
        compiler_params=params(2),
        cost_estimate=cost(1),
        name="join",
    )(x, *after)


def attention_kernel(
    sc_ref,
    qd_ref,
    kv0_ref,
    kv1_ref,
    kv2_ref,
    kv3_ref,
    dq_ref,
    own_ref,
    core_ref,
    far_ref,
    farcore_ref,
    tok_ref,
    k_s,
    v_s,
    kt_s,
    q_s,
    do_s,
    e_s,
    w_s,
    p_s,
    dk_s,
    dv_s,
    tot,
    mom,
    dqt,
    perm,
    dot_s,
):
    prefix, zh, core = sc_ref[0], sc_ref[1], sc_ref[2]
    eye = (
        lax.broadcasted_iota(jnp.int32, (HD, HD), 0) == lax.broadcasted_iota(jnp.int32, (HD, HD), 1)
    ).astype(bf16)
    for seg in range(NSEG):
        near, away = ((kv0_ref, kv1_ref), (kv2_ref, kv3_ref))[seg // 4]
        y = seg % 4
        whole = jnp.concatenate([near[2 * y], near[2 * y + 1], away[2 * y], away[2 * y + 1]], 0)
        k_s[seg] = whole[:, :HD]
        v_s[seg] = whole[:, HD:]
        kt_s[seg] = mm(eye, whole[:, :HD], NT).astype(bf16)
    dk_s[...] = jnp.zeros_like(dk_s)
    dv_s[...] = jnp.zeros_like(dv_s)

    def key_start(j):
        far = j // 4
        return (j % 4) * 1024 + (zh + far - 2 * zh * far) * SEG

    def hidden(key0, row0):
        s = lax.broadcasted_iota(jnp.int32, (SEG, SEG), 0)
        piece = s // TOK
        other = piece // 2
        key = key0 + (piece % 2) * 256 + (core + other - 2 * core * other) * TOK + s % TOK
        lane = lax.broadcasted_iota(jnp.int32, (1, SEG), 1)
        row = row0 + ((lane // TOK) % 2) * 256 + lane % TOK
        return key >= jnp.maximum(row + 1, prefix)

    def row_body(i, _):
        row0 = i * 1024 + zh * SEG + core * TOK
        limit = jnp.maximum(prefix, row0 + 384)
        full = jnp.maximum(prefix, row0 + 1)
        for head in range(2):
            for z in range(2):
                at = pl.ds((head * 2 + z) * TOK, TOK)
                q_s[at, :] = qd_ref[2 * i + z, :, head * HD : (head + 1) * HD]
                do_s[at, :] = qd_ref[2 * i + z, :, (2 + head) * HD : (3 + head) * HD]
        tot[...] = jnp.zeros_like(tot)
        mom[...] = jnp.zeros_like(mom)
        dqt[...] = jnp.zeros_like(dqt)

        def scores(y, masked):
            pair = (y, y + 4)
            for j in pair:
                for c in range(0, SEG, 256):
                    cc = slice(c, c + 256)
                    t = jnp.tanh(mm(k_s[j], q_s[cc, :], NT) * tanh_scale)
                    dp = mm(v_s[j], do_s[cc, :], NT)
                    e = jnp.exp2(t * exp2_scale)
                    if masked:
                        e = jnp.where(hidden(key_start(j), row0)[:, cc], 0.0, e)
                    tot[:, cc] += jnp.sum(e, 0, keepdims=True)
                    mom[:, cc] += jnp.sum(e * dp, 0, keepdims=True)
                    e_s[j, :, cc] = e.astype(bf16)
                    w_s[j, :, cc] = e * (1.0 - t * t)
                    p_s[j, :, cc] = dp

        def first(y, _):
            @pl.when(y * 1024 + 1024 <= full)
            def _():
                scores(y, False)

            @pl.when((y * 1024 + 1024 > full) & (y * 1024 < limit))
            def _():
                scores(y, True)

            return 0

        lax.fori_loop(0, 4, first, 0)
        inv = 1.0 / tot[...]
        delta = mom[...] * inv
        dot_s[...] = (mm(eye, do_s[...], NT) * inv).astype(bf16)

        def second(y, _):
            @pl.when(y * 1024 < limit)
            def _():
                grad = dqt[...]
                for j in (y, y + 4):
                    ds = (w_s[j] * inv * (p_s[j] - delta)).astype(bf16)
                    dv_s[j] += mm(e_s[j], dot_s[...], NT)
                    dk_s[j] += mm(ds, q_s[...])
                    grad += mm(kt_s[j], ds)
                dqt[...] = grad

            return 0

        lax.fori_loop(0, 4, second, 0)
        dq = (dqt[...] * score_scale).T.astype(bf16)
        for head in range(2):
            for z in range(2):
                at = (head * 2 + z) * TOK
                dq_ref[2 * i + z, :, head * HD : (head + 1) * HD] = dq[at : at + TOK]
        return 0

    lax.fori_loop(0, 4, row_body, 0)

    out = lax.broadcasted_iota(jnp.int32, (SEG, SEG), 0)
    src = lax.broadcasted_iota(jnp.int32, (SEG, SEG), 1)
    slot = out % 16
    c_of = (slot // 4) % 2
    want = (
        (c_of + core - 2 * c_of * core) * 256 + (slot // 8) * TOK + (slot % 4) * 32 + out // 16
    )
    perm[...] = (want == src).astype(bf16)
    for seg in range(NSEG):
        near, away = ((own_ref, core_ref), (far_ref, farcore_ref))[seg // 4]
        y = seg % 4
        terms = jnp.concatenate([dk_s[seg] * score_scale, dv_s[seg]], 1)
        near[2 * y] = terms[:TOK].astype(near.dtype)
        near[2 * y + 1] = terms[TOK : 2 * TOK].astype(near.dtype)
        away[2 * y] = terms[2 * TOK : 3 * TOK].astype(away.dtype)
        away[2 * y + 1] = terms[3 * TOK :].astype(away.dtype)
        if y < 2:
            moved = mm(perm[...], terms.astype(bf16)).astype(bf16).reshape(32, 16, 2 * HD)
            z_at = zh if seg < 4 else 1 - zh
            tok_ref[:, pl.ds(pl.multiple_of((2 * y + z_at) * 16, 16), 16), :] = moved


def attention(sc, qd, kv0, kv1, kv2, kv3):
    part = (KVH, TOK, 2 * HD)
    return pl.pallas_call(
        attention_kernel,
        out_shape=(
            jax.ShapeDtypeStruct(part, bf16),
            jax.ShapeDtypeStruct(part, f32),
            jax.ShapeDtypeStruct(part, bf16),
            jax.ShapeDtypeStruct(part, bf16),
            jax.ShapeDtypeStruct(part, bf16),
            jax.ShapeDtypeStruct((32, SLOTS, 2 * HD), bf16),
        ),
        in_specs=[SM] + [VM] * 5,
        out_specs=(VM,) * 6,
        scratch_shapes=[
            pltpu.VMEM((NSEG, SEG, HD), bf16),
            pltpu.VMEM((NSEG, SEG, HD), bf16),
            pltpu.VMEM((NSEG, HD, SEG), bf16),
            pltpu.VMEM((SEG, HD), bf16),
            pltpu.VMEM((SEG, HD), bf16),
            pltpu.VMEM((NSEG, SEG, SEG), bf16),
            pltpu.VMEM((NSEG, SEG, SEG), f32),
            pltpu.VMEM((NSEG, SEG, SEG), f32),
            pltpu.VMEM((NSEG, SEG, HD), f32),
            pltpu.VMEM((NSEG, SEG, HD), f32),
            pltpu.VMEM((1, SEG), f32),
            pltpu.VMEM((1, SEG), f32),
            pltpu.VMEM((HD, SEG), f32),
            pltpu.VMEM((SEG, SEG), bf16),
            pltpu.VMEM((HD, SEG), bf16),
        ],
        compiler_params=params(60),
        cost_estimate=cost(36),
        name="attention",
    )(sc, qd, kv0, kv1, kv2, kv3)


def pair_sum_kernel(a_ref, b_ref, out_ref):
    out_ref[...] = (a_ref[...].astype(f32) + b_ref[...].astype(f32)).astype(bf16)


def pair_sum(a, b):
    return pl.pallas_call(
        pair_sum_kernel,
        out_shape=jax.ShapeDtypeStruct(a.shape, bf16),
        in_specs=[VM, VM],
        out_specs=VM,
        compiler_params=params(60),
        cost_estimate=cost(2, 3_000_000_000),
        name="pair_sum",
    )(a, b)


def last_sum_kernel(dq_ref, a_ref, b_ref, c_ref, _, out_ref):
    out_ref[:, :, : 2 * HD] = dq_ref[...]
    total = a_ref[...] + b_ref[...].astype(f32) + c_ref[...].astype(f32)
    out_ref[:, :, 2 * HD :] = total.astype(bf16)


def last_sum(dq, a, b, c, after):
    return pl.pallas_call(
        last_sum_kernel,
        out_shape=jax.ShapeDtypeStruct((KVH, TOK, 4 * HD), bf16),
        in_specs=[VM] * 4 + [ANY],
        out_specs=VM,
        compiler_params=params(8),
        cost_estimate=cost(3),
        name="last_sum",
    )(dq, a, b, c, after)


def unpack_kernel(half_ref, in_ref, q_ref, k_ref, v_ref):
    for h in range(KVH):
        at = (h // 2) * 2 + (h % 2 + half_ref[0] - 2 * (h % 2) * half_ref[0])
        q_ref[:, h * 2 * HD : (h + 1) * 2 * HD] = in_ref[at, :, : 2 * HD]
        k_ref[:, h * HD : (h + 1) * HD] = in_ref[at, :, 2 * HD : 3 * HD]
        v_ref[:, h * HD : (h + 1) * HD] = in_ref[at, :, 3 * HD :]


def unpack(half, grads):
    return pl.pallas_call(
        unpack_kernel,
        out_shape=(
            jax.ShapeDtypeStruct((TOK, 2 * KVH * HD), bf16),
            jax.ShapeDtypeStruct((TOK, KVH * HD), bf16),
            jax.ShapeDtypeStruct((TOK, KVH * HD), bf16),
        ),
        in_specs=[SM, VM],
        out_specs=(VM, VM, VM),
        compiler_params=params(8),
        cost_estimate=cost(2),
        name="unpack",
    )(half, grads)


def token_kernel(sc_ref, tok_ref, u0, u1, u2, u3, out_ref):
    token = lax.broadcasted_iota(jnp.int32, (SLOTS, 2 * HD), 0) * 32 + sc_ref[4]
    visible = token < sc_ref[3]
    wide = KVH * HD
    cross = jnp.zeros((SLOTS, 1), f32)
    for h in range(KVH):
        base = (h // 2) * 8 + (h % 2) * 2
        away = (h // 2) * 8 + 4 + (1 - h % 2) * 2
        total = tok_ref[base].astype(f32) + tok_ref[base + 1].astype(f32)
        total = total + tok_ref[away].astype(f32) + tok_ref[away + 1].astype(f32)
        total = jnp.where(visible, total, 0.0).astype(bf16)
        for half in range(2):
            at = slice(half * wide + h * HD, half * wide + (h + 1) * HD)
            part = total[:, half * HD : (half + 1) * HD]
            out_ref[:, at] = part
            mixed = u0[:, at].astype(f32) + u1[:, at].astype(f32)
            mixed = mixed + u2[:, at].astype(f32) + u3[:, at].astype(f32)
            cross += jnp.sum(part.astype(f32) * mixed, 1, keepdims=True)
    lane = lax.broadcasted_iota(jnp.int32, (SLOTS, 128), 1)
    tail = u0[:, 2 * wide :].astype(f32) + u1[:, 2 * wide :].astype(f32)
    tail = tail + u2[:, 2 * wide :].astype(f32) + u3[:, 2 * wide :].astype(f32)
    sq = jnp.sum(tail, 1, keepdims=True)
    parts = split3(lax.rsqrt(sq / D + norm_eps)) + split3(cross / D)
    tail = jnp.zeros((SLOTS, 128), f32)
    for n, part in enumerate(parts):
        tail = jnp.where(lane == n, part.astype(f32), tail)
    out_ref[:, 2 * wide :] = tail.astype(bf16)


def token_rows(sc, tok, mixed):
    return pl.pallas_call(
        token_kernel,
        out_shape=jax.ShapeDtypeStruct((SLOTS, 2 * KVH * HD + 128), bf16),
        in_specs=[SM] + [VM] * 5,
        out_specs=VM,
        compiler_params=params(60),
        cost_estimate=cost(2),
        name="token_rows",
    )(sc, tok, *mixed)


def image_kernel(
    sc_ref, owner_ref, r0, r1, r2, r3, wk_ref, wv_ref, embed_ref, scale_ref, out_ref, wk_s, wv_s, sems
):
    at = pl.ds(pl.multiple_of(sc_ref[5] * FS, FS), FS)
    copies = (
        pltpu.make_async_copy(wk_ref.at[at], wk_s, sems.at[0]),
        pltpu.make_async_copy(wv_ref.at[at], wv_s, sems.at[1]),
    )
    for copy in copies:
        copy.start()
    wide = KVH * HD
    recvs = (r0, r1, r2, r3)
    xk = jnp.concatenate([r[:, :wide] for r in recvs], 0)
    xv = jnp.concatenate([r[:, wide : 2 * wide] for r in recvs], 0)
    copies[0].wait()
    projected = mm(xk, wk_s[...], NT)
    copies[1].wait()
    projected = projected + mm(xv, wv_s[...], NT)
    lane = lax.broadcasted_iota(jnp.int32, (SLOTS, 128), 1)
    scale = scale_ref[...].reshape(1, FS)
    for n, recv_ref in enumerate(recvs):
        row = owner_ref[n]
        tail = recv_ref[:, 2 * wide :].astype(f32)
        inv = jnp.sum(jnp.where(lane < 3, tail, 0.0), 1, keepdims=True)
        cross = jnp.sum(jnp.where(lane >= 3, tail, 0.0), 1, keepdims=True)
        grad = projected[n * SLOTS : (n + 1) * SLOTS].astype(bf16).astype(f32)
        rows = embed_ref[row].astype(f32)
        out_ref[row] = inv * (scale * grad) - rows * (inv * inv * inv * cross)


def image_out(sc, owner, recvs, wk, wv, embed, scale):
    return pl.pallas_call(
        image_kernel,
        out_shape=jax.ShapeDtypeStruct((NDP, SLOTS, FS), f32),
        in_specs=[SM, SM] + [VM] * 4 + [ANY, ANY, VM, VM],
        out_specs=VM,
        scratch_shapes=[
            pltpu.VMEM((FS, KVH * HD), bf16),
            pltpu.VMEM((FS, KVH * HD), bf16),
            pltpu.SemaphoreType.DMA((2,)),
        ],
        compiler_params=params(60),
        cost_estimate=cost(5, 60_000_000_000),
        name="image_out",
    )(sc, owner, *recvs, wk, wv, embed, scale)


def exchange(x, axes):
    return lax.all_to_all(x, axes, split_axis=0, concat_axis=0, tiled=True)


def shift(x, by):
    return lax.ppermute(x, "dp", [(i, (i + by) % NDP) for i in range(NDP)])


def mirror(x):
    return lax.ppermute(x, ("zh", "zl"), [(i, 3 - i) for i in range(4)])


def swap(x, axis):
    return lax.ppermute(x, axis, [(0, 1), (1, 0)])


def local(
    query_states,
    key_states,
    value_states,
    out_grads,
    image_counts,
    prefix_lengths,
    encoder_owner,
    key_weight,
    value_weight,
    norm_scale,
    image_embed,
):
    ctx = ("y", "zh", "zl", "core")
    dp = lax.axis_index("dp")
    half = lax.axis_index("zh").astype(jnp.int32).reshape(1)
    sc = jnp.stack(
        [
            prefix_lengths[0],
            lax.axis_index("zh"),
            lax.axis_index("core"),
            image_counts[0],
            lax.axis_index(ctx),
            dp,
        ]
    ).astype(jnp.int32)
    owner = lax.dynamic_slice(jnp.concatenate([encoder_owner, encoder_owner]), (dp,), (NDP,))

    kv0 = exchange(pack_heads(half, key_states[0], value_states[0], "pack_kv"), ("y", "zl"))
    qd_pack = pack_heads(half, query_states[0], out_grads[0], "pack_qd")
    mark, *mixed = mix(sc, owner, image_embed, norm_scale, key_weight, value_weight)
    kv0 = join(kv0, mark, qd_pack)
    kv1 = swap(kv0, "core")
    mixed = [mixed[0]] + [shift(mixed[n], n) for n in range(1, NDP)]
    kv2 = join(mirror(kv0), mixed[1], mixed[3])
    kv3 = swap(kv2, "core")
    qd = exchange(qd_pack, ("y", "zl"))

    dq, own, core_part, far, farcore, tok = attention(sc, qd, kv0, kv1, kv2, kv3)

    tok_in = exchange(tok, ctx)
    far_sum = pair_sum(far, swap(farcore, "core"))
    rows = token_rows(sc, tok_in, mixed)
    grads = last_sum(dq, own, swap(core_part, "core"), mirror(far_sum), rows)
    recvs = [rows] + [shift(rows, -n) for n in range(1, NDP)]
    image_grads = image_out(
        sc, owner, recvs, key_weight, value_weight, image_embed, norm_scale
    )
    query_grads, key_grads, value_grads = unpack(half, exchange(grads, ("y", "zl")))
    return (query_grads[None], key_grads[None], value_grads[None], image_grads)


def solution(mesh):
    ctx = ("y", "zh", "zl", "core")
    split = Mesh(mesh.devices.reshape(4, 4, 2, 2, 2), ("dp",) + ctx)
    rows = P("dp", ctx, None)
    image = P(None, ctx, "dp")
    in_specs = (rows, rows, rows, rows, P("dp"), P("dp"), P(), P(), P(), P("dp"), image)
    out_specs = (rows, rows, rows, image)
    return jax.shard_map(local, mesh=split, in_specs=in_specs, out_specs=out_specs, check_vma=False)
```

```python
import functools
import math

import jax
import jax.numpy as jnp
from jax import lax
from jax.experimental import pallas as pl
from jax.experimental.pallas import tpu as pltpu
from jax.sharding import Mesh, PartitionSpec as P

D = 4608
HD = 128
KVH = 8
TOK = 128
SLOTS = 64
NDP = 4
FS = D // NDP
SEG = 512
NSEG = 8

score_scale = 144.0 ** (-0.5)
soft_cap = 50.0
norm_eps = 1e-06
tanh_scale = score_scale / soft_cap
exp2_scale = soft_cap * math.log2(math.e)

f32 = jnp.float32
bf16 = jnp.bfloat16
VM = pl.BlockSpec(memory_space=pltpu.VMEM)
ANY = pl.BlockSpec(memory_space=pl.ANY)
SM = pl.BlockSpec(memory_space=pltpu.SMEM)
NT = (((1,), (1,)), ((), ()))
NN = (((1,), (0,)), ((), ()))


def mm(a, b, dims=NN):
    return lax.dot_general(a, b, dims, preferred_element_type=f32)


def split3(x):
    hi = x.astype(bf16)
    rest = x - hi.astype(f32)
    mid = rest.astype(bf16)
    lo = (rest - mid.astype(f32)).astype(bf16)
    return hi, mid, lo


def params(mib):
    return pltpu.CompilerParams(vmem_limit_bytes=mib << 20)


def cost(us, flops=0):
    return pl.CostEstimate(flops=flops, bytes_accessed=int(us * 3_000_000), transcendentals=0)


def pack_kernel(width, half_ref, a_ref, b_ref, out_ref):
    for h in range(KVH):
        at = (h // 2) * 2 + (h % 2 + half_ref[0] - 2 * (h % 2) * half_ref[0])
        out_ref[at, :, :width] = a_ref[:, h * width : (h + 1) * width]
        out_ref[at, :, width:] = b_ref[:, h * width : (h + 1) * width]


def pack_heads(half, a, b, name):
    width = a.shape[1] // KVH
    return pl.pallas_call(
        functools.partial(pack_kernel, width),
        out_shape=jax.ShapeDtypeStruct((KVH, TOK, 2 * width), bf16),
        in_specs=[SM, VM, VM],
        out_specs=VM,
        compiler_params=params(60),
        cost_estimate=cost(2),
        name=name,
    )(half, a, b)


def mixed_kernel(
    sc_ref, owner_ref, embed_ref, scale_ref, wk_ref, wv_ref, mark_ref, u0, u1, u2, u3, wk_s, wv_s, sems
):
    at = pl.ds(pl.multiple_of(sc_ref[5] * FS, FS), FS)
    copies = (
        pltpu.make_async_copy(wk_ref.at[at], wk_s, sems.at[0]),
        pltpu.make_async_copy(wv_ref.at[at], wv_s, sems.at[1]),
    )
    for copy in copies:
        copy.start()
    mark_ref[...] = jnp.zeros_like(mark_ref)
    lane = lax.broadcasted_iota(jnp.int32, (SLOTS, 128), 1)
    scale = scale_ref[...].reshape(1, FS)
    outs = (u0, u1, u2, u3)
    scaled = []
    for n in range(NDP):
        rows = embed_ref[owner_ref[n]].astype(f32)
        tail = jnp.zeros((SLOTS, 128), f32)
        for k, part in enumerate(split3(jnp.sum(rows * rows, 1, keepdims=True))):
            tail = jnp.where(lane == k, part.astype(f32), tail)
        outs[n][:, 2 * KVH * HD :] = tail.astype(bf16)
        scaled.append((rows * scale).astype(bf16))
    scaled = jnp.concatenate(scaled, 0)
    for half, (copy, w_s) in enumerate(zip(copies, (wk_s, wv_s))):
        copy.wait()
        mixed = mm(scaled, w_s[...]).astype(bf16)
        for n in range(NDP):
            outs[n][:, half * KVH * HD : (half + 1) * KVH * HD] = mixed[
                n * SLOTS : (n + 1) * SLOTS
            ]


def mix(sc, owner, embed, scale, wk, wv):
    one = jax.ShapeDtypeStruct((SLOTS, 2 * KVH * HD + 128), bf16)
    return pl.pallas_call(
        mixed_kernel,
        out_shape=(jax.ShapeDtypeStruct((8, 128), f32),) + (one,) * NDP,
        in_specs=[SM, SM, VM, VM, ANY, ANY],
        out_specs=(VM,) * (NDP + 1),
        scratch_shapes=[
            pltpu.VMEM((FS, KVH * HD), bf16),
            pltpu.VMEM((FS, KVH * HD), bf16),
            pltpu.SemaphoreType.DMA((2,)),
        ],
        compiler_params=params(60),
        cost_estimate=cost(5),
        name="mix",
    )(sc, owner, embed, scale, wk, wv)


def join(x, *after):
    return pl.pallas_call(
        lambda *refs: None,
        out_shape=jax.ShapeDtypeStruct(x.shape, x.dtype),
        in_specs=[ANY] * (1 + len(after)),
        out_specs=ANY,
        input_output_aliases={0: 0},
        compiler_params=params(2),
        cost_estimate=cost(1),
        name="join",
    )(x, *after)


def attention_kernel(
    sc_ref,
    qd_ref,
    kv0_ref,
    kv1_ref,
    kv2_ref,
    kv3_ref,
    dq_ref,
    own_ref,
    core_ref,
    far_ref,
    farcore_ref,
    tok_ref,
    k_s,
    v_s,
    kt_s,
    q_s,
    do_s,
    e_s,
    w_s,
    p_s,
    dk_s,
    dv_s,
    tot,
    mom,
    dqt,
    perm,
    dot_s,
):
    prefix, zh, core = sc_ref[0], sc_ref[1], sc_ref[2]
    eye = (
        lax.broadcasted_iota(jnp.int32, (HD, HD), 0) == lax.broadcasted_iota(jnp.int32, (HD, HD), 1)
    ).astype(bf16)
    for seg in range(NSEG):
        near, away = ((kv0_ref, kv1_ref), (kv2_ref, kv3_ref))[seg // 4]
        y = seg % 4
        whole = jnp.concatenate([near[2 * y], near[2 * y + 1], away[2 * y], away[2 * y + 1]], 0)
        k_s[seg] = whole[:, :HD]
        v_s[seg] = whole[:, HD:]
        kt_s[seg] = mm(eye, whole[:, :HD], NT).astype(bf16)
    dk_s[...] = jnp.zeros_like(dk_s)
    dv_s[...] = jnp.zeros_like(dv_s)

    def key_start(j):
        far = j // 4
        return (j % 4) * 1024 + (zh + far - 2 * zh * far) * SEG

    def hidden(key0, row0):
        s = lax.broadcasted_iota(jnp.int32, (SEG, SEG), 0)
        piece = s // TOK
        other = piece // 2
        key = key0 + (piece % 2) * 256 + (core + other - 2 * core * other) * TOK + s % TOK
        lane = lax.broadcasted_iota(jnp.int32, (1, SEG), 1)
        row = row0 + ((lane // TOK) % 2) * 256 + lane % TOK
        return key >= jnp.maximum(row + 1, prefix)

    def row_body(i, _):
        row0 = i * 1024 + zh * SEG + core * TOK
        limit = jnp.maximum(prefix, row0 + 384)
        full = jnp.maximum(prefix, row0 + 1)
        for head in range(2):
            for z in range(2):
                at = pl.ds((head * 2 + z) * TOK, TOK)
                q_s[at, :] = qd_ref[2 * i + z, :, head * HD : (head + 1) * HD]
                do_s[at, :] = qd_ref[2 * i + z, :, (2 + head) * HD : (3 + head) * HD]
        tot[...] = jnp.zeros_like(tot)
        mom[...] = jnp.zeros_like(mom)
        dqt[...] = jnp.zeros_like(dqt)

        def scores(y, masked):
            pair = (y, y + 4)
            for j in pair:
                for c in range(0, SEG, 256):
                    cc = slice(c, c + 256)
                    t = jnp.tanh(mm(k_s[j], q_s[cc, :], NT) * tanh_scale)
                    dp = mm(v_s[j], do_s[cc, :], NT)
                    e = jnp.exp2(t * exp2_scale)
                    if masked:
                        e = jnp.where(hidden(key_start(j), row0)[:, cc], 0.0, e)
                    tot[:, cc] += jnp.sum(e, 0, keepdims=True)
                    mom[:, cc] += jnp.sum(e * dp, 0, keepdims=True)
                    e_s[j, :, cc] = e.astype(bf16)
                    w_s[j, :, cc] = e * (1.0 - t * t)
                    p_s[j, :, cc] = dp

        def first(y, _):
            @pl.when(y * 1024 + 1024 <= full)
            def _():
                scores(y, False)

            @pl.when((y * 1024 + 1024 > full) & (y * 1024 < limit))
            def _():
                scores(y, True)

            return 0

        lax.fori_loop(0, 4, first, 0)
        inv = 1.0 / tot[...]
        delta = mom[...] * inv
        dot_s[...] = (mm(eye, do_s[...], NT) * inv).astype(bf16)

        def second(y, _):
            @pl.when(y * 1024 < limit)
            def _():
                grad = dqt[...]
                for j in (y, y + 4):
                    ds = (w_s[j] * inv * (p_s[j] - delta)).astype(bf16)
                    dv_s[j] += mm(e_s[j], dot_s[...], NT)
                    dk_s[j] += mm(ds, q_s[...])
                    grad += mm(kt_s[j], ds)
                dqt[...] = grad

            return 0

        lax.fori_loop(0, 4, second, 0)
        dq = (dqt[...] * score_scale).T.astype(bf16)
        for head in range(2):
            for z in range(2):
                at = (head * 2 + z) * TOK
                dq_ref[2 * i + z, :, head * HD : (head + 1) * HD] = dq[at : at + TOK]
        return 0

    lax.fori_loop(0, 4, row_body, 0)

    out = lax.broadcasted_iota(jnp.int32, (SEG, SEG), 0)
    src = lax.broadcasted_iota(jnp.int32, (SEG, SEG), 1)
    slot = out % 16
    c_of = (slot // 4) % 2
    want = (
        (c_of + core - 2 * c_of * core) * 256 + (slot // 8) * TOK + (slot % 4) * 32 + out // 16
    )
    perm[...] = (want == src).astype(bf16)
    for seg in range(NSEG):
        near, away = ((own_ref, core_ref), (far_ref, farcore_ref))[seg // 4]
        y = seg % 4
        terms = jnp.concatenate([dk_s[seg] * score_scale, dv_s[seg]], 1)
        near[2 * y] = terms[:TOK].astype(near.dtype)
        near[2 * y + 1] = terms[TOK : 2 * TOK].astype(near.dtype)
        away[2 * y] = terms[2 * TOK : 3 * TOK].astype(away.dtype)
        away[2 * y + 1] = terms[3 * TOK :].astype(away.dtype)
        if y < 2:
            moved = mm(perm[...], terms.astype(bf16)).astype(bf16).reshape(32, 16, 2 * HD)
            z_at = zh if seg < 4 else 1 - zh
            tok_ref[:, pl.ds(pl.multiple_of((2 * y + z_at) * 16, 16), 16), :] = moved


def attention(sc, qd, kv0, kv1, kv2, kv3):
    part = (KVH, TOK, 2 * HD)
    return pl.pallas_call(
        attention_kernel,
        out_shape=(
            jax.ShapeDtypeStruct(part, bf16),
            jax.ShapeDtypeStruct(part, f32),
            jax.ShapeDtypeStruct(part, bf16),
            jax.ShapeDtypeStruct(part, bf16),
            jax.ShapeDtypeStruct(part, bf16),
            jax.ShapeDtypeStruct((32, SLOTS, 2 * HD), bf16),
        ),
        in_specs=[SM] + [VM] * 5,
        out_specs=(VM,) * 6,
        scratch_shapes=[
            pltpu.VMEM((NSEG, SEG, HD), bf16),
            pltpu.VMEM((NSEG, SEG, HD), bf16),
            pltpu.VMEM((NSEG, HD, SEG), bf16),
            pltpu.VMEM((SEG, HD), bf16),
            pltpu.VMEM((SEG, HD), bf16),
            pltpu.VMEM((NSEG, SEG, SEG), bf16),
            pltpu.VMEM((NSEG, SEG, SEG), f32),
            pltpu.VMEM((NSEG, SEG, SEG), f32),
            pltpu.VMEM((NSEG, SEG, HD), f32),
            pltpu.VMEM((NSEG, SEG, HD), f32),
            pltpu.VMEM((1, SEG), f32),
            pltpu.VMEM((1, SEG), f32),
            pltpu.VMEM((HD, SEG), f32),
            pltpu.VMEM((SEG, SEG), bf16),
            pltpu.VMEM((HD, SEG), bf16),
        ],
        compiler_params=params(60),
        cost_estimate=cost(36),
        name="attention",
    )(sc, qd, kv0, kv1, kv2, kv3)


def pair_sum_kernel(a_ref, b_ref, out_ref):
    out_ref[...] = (a_ref[...].astype(f32) + b_ref[...].astype(f32)).astype(bf16)


def pair_sum(a, b):
    return pl.pallas_call(
        pair_sum_kernel,
        out_shape=jax.ShapeDtypeStruct(a.shape, bf16),
        in_specs=[VM, VM],
        out_specs=VM,
        compiler_params=params(8),
        cost_estimate=cost(2, 3_000_000_000),
        name="pair_sum",
    )(a, b)


def last_sum_kernel(dq_ref, a_ref, b_ref, c_ref, out_ref):
    out_ref[:, :, : 2 * HD] = dq_ref[...]
    total = a_ref[...] + b_ref[...].astype(f32) + c_ref[...].astype(f32)
    out_ref[:, :, 2 * HD :] = total.astype(bf16)


def last_sum(dq, a, b, c):
    return pl.pallas_call(
        last_sum_kernel,
        out_shape=jax.ShapeDtypeStruct((KVH, TOK, 4 * HD), bf16),
        in_specs=[VM] * 4,
        out_specs=VM,
        compiler_params=params(8),
        cost_estimate=cost(3),
        name="last_sum",
    )(dq, a, b, c)


def unpack_kernel(half_ref, in_ref, q_ref, k_ref, v_ref):
    for h in range(KVH):
        at = (h // 2) * 2 + (h % 2 + half_ref[0] - 2 * (h % 2) * half_ref[0])
        q_ref[:, h * 2 * HD : (h + 1) * 2 * HD] = in_ref[at, :, : 2 * HD]
        k_ref[:, h * HD : (h + 1) * HD] = in_ref[at, :, 2 * HD : 3 * HD]
        v_ref[:, h * HD : (h + 1) * HD] = in_ref[at, :, 3 * HD :]


def unpack(half, grads):
    return pl.pallas_call(
        unpack_kernel,
        out_shape=(
            jax.ShapeDtypeStruct((TOK, 2 * KVH * HD), bf16),
            jax.ShapeDtypeStruct((TOK, KVH * HD), bf16),
            jax.ShapeDtypeStruct((TOK, KVH * HD), bf16),
        ),
        in_specs=[SM, VM],
        out_specs=(VM, VM, VM),
        compiler_params=params(8),
        cost_estimate=cost(2),
        name="unpack",
    )(half, grads)


def token_kernel(sc_ref, tok_ref, u0, u1, u2, u3, out_ref):
    token = lax.broadcasted_iota(jnp.int32, (SLOTS, 2 * HD), 0) * 32 + sc_ref[4]
    visible = token < sc_ref[3]
    wide = KVH * HD
    cross = jnp.zeros((SLOTS, 1), f32)
    for h in range(KVH):
        base = (h // 2) * 8 + (h % 2) * 2
        away = (h // 2) * 8 + 4 + (1 - h % 2) * 2
        total = tok_ref[base].astype(f32) + tok_ref[base + 1].astype(f32)
        total = total + tok_ref[away].astype(f32) + tok_ref[away + 1].astype(f32)
        total = jnp.where(visible, total, 0.0).astype(bf16)
        for half in range(2):
            at = slice(half * wide + h * HD, half * wide + (h + 1) * HD)
            part = total[:, half * HD : (half + 1) * HD]
            out_ref[:, at] = part
            mixed = u0[:, at].astype(f32) + u1[:, at].astype(f32)
            mixed = mixed + u2[:, at].astype(f32) + u3[:, at].astype(f32)
            cross += jnp.sum(part.astype(f32) * mixed, 1, keepdims=True)
    lane = lax.broadcasted_iota(jnp.int32, (SLOTS, 128), 1)
    tail = u0[:, 2 * wide :].astype(f32) + u1[:, 2 * wide :].astype(f32)
    tail = tail + u2[:, 2 * wide :].astype(f32) + u3[:, 2 * wide :].astype(f32)
    sq = jnp.sum(tail, 1, keepdims=True)
    parts = split3(lax.rsqrt(sq / D + norm_eps)) + split3(cross / D)
    tail = jnp.zeros((SLOTS, 128), f32)
    for n, part in enumerate(parts):
        tail = jnp.where(lane == n, part.astype(f32), tail)
    out_ref[:, 2 * wide :] = tail.astype(bf16)


def token_rows(sc, tok, mixed):
    return pl.pallas_call(
        token_kernel,
        out_shape=jax.ShapeDtypeStruct((SLOTS, 2 * KVH * HD + 128), bf16),
        in_specs=[SM] + [VM] * 5,
        out_specs=VM,
        compiler_params=params(60),
        cost_estimate=cost(2),
        name="token_rows",
    )(sc, tok, *mixed)


def image_kernel(
    sc_ref, owner_ref, r0, r1, r2, r3, wk_ref, wv_ref, embed_ref, scale_ref, out_ref, wk_s, wv_s, sems
):
    at = pl.ds(pl.multiple_of(sc_ref[5] * FS, FS), FS)
    copies = (
        pltpu.make_async_copy(wk_ref.at[at], wk_s, sems.at[0]),
        pltpu.make_async_copy(wv_ref.at[at], wv_s, sems.at[1]),
    )
    for copy in copies:
        copy.start()
    wide = KVH * HD
    recvs = (r0, r1, r2, r3)
    xk = jnp.concatenate([r[:, :wide] for r in recvs], 0)
    xv = jnp.concatenate([r[:, wide : 2 * wide] for r in recvs], 0)
    copies[0].wait()
    projected = mm(xk, wk_s[...], NT)
    copies[1].wait()
    projected = projected + mm(xv, wv_s[...], NT)
    lane = lax.broadcasted_iota(jnp.int32, (SLOTS, 128), 1)
    scale = scale_ref[...].reshape(1, FS)
    for n, recv_ref in enumerate(recvs):
        row = owner_ref[n]
        tail = recv_ref[:, 2 * wide :].astype(f32)
        inv = jnp.sum(jnp.where(lane < 3, tail, 0.0), 1, keepdims=True)
        cross = jnp.sum(jnp.where(lane >= 3, tail, 0.0), 1, keepdims=True)
        grad = projected[n * SLOTS : (n + 1) * SLOTS].astype(bf16).astype(f32)
        rows = embed_ref[row].astype(f32)
        out_ref[row] = inv * (scale * grad) - rows * (inv * inv * inv * cross)


def image_out(sc, owner, recvs, wk, wv, embed, scale):
    return pl.pallas_call(
        image_kernel,
        out_shape=jax.ShapeDtypeStruct((NDP, SLOTS, FS), f32),
        in_specs=[SM, SM] + [VM] * 4 + [ANY, ANY, VM, VM],
        out_specs=VM,
        scratch_shapes=[
            pltpu.VMEM((FS, KVH * HD), bf16),
            pltpu.VMEM((FS, KVH * HD), bf16),
            pltpu.SemaphoreType.DMA((2,)),
        ],
        compiler_params=params(60),
        cost_estimate=cost(5, 60_000_000_000),
        name="image_out",
    )(sc, owner, *recvs, wk, wv, embed, scale)


def exchange(x, axes):
    return lax.all_to_all(x, axes, split_axis=0, concat_axis=0, tiled=True)


def shift(x, by):
    return lax.ppermute(x, "dp", [(i, (i + by) % NDP) for i in range(NDP)])


def mirror(x):
    return lax.ppermute(x, ("zh", "zl"), [(i, 3 - i) for i in range(4)])


def swap(x, axis):
    return lax.ppermute(x, axis, [(0, 1), (1, 0)])


def local(
    query_states,
    key_states,
    value_states,
    out_grads,
    image_counts,
    prefix_lengths,
    encoder_owner,
    key_weight,
    value_weight,
    norm_scale,
    image_embed,
):
    ctx = ("y", "zh", "zl", "core")
    dp = lax.axis_index("dp")
    half = lax.axis_index("zh").astype(jnp.int32).reshape(1)
    sc = jnp.stack(
        [
            prefix_lengths[0],
            lax.axis_index("zh"),
            lax.axis_index("core"),
            image_counts[0],
            lax.axis_index(ctx),
            dp,
        ]
    ).astype(jnp.int32)
    owner = lax.dynamic_slice(jnp.concatenate([encoder_owner, encoder_owner]), (dp,), (NDP,))

    kv0 = exchange(pack_heads(half, key_states[0], value_states[0], "pack_kv"), ("y", "zl"))
    qd_pack = pack_heads(half, query_states[0], out_grads[0], "pack_qd")
    mark, *mixed = mix(sc, owner, image_embed, norm_scale, key_weight, value_weight)
    kv0 = join(kv0, mark, qd_pack)
    kv1 = swap(kv0, "core")
    mixed = [mixed[0]] + [shift(mixed[n], n) for n in range(1, NDP)]
    kv2 = join(mirror(kv0), mixed[1], mixed[3])
    kv3 = swap(kv2, "core")
    qd = exchange(qd_pack, ("y", "zl"))

    dq, own, core_part, far, farcore, tok = attention(sc, qd, kv0, kv1, kv2, kv3)

    tok_in = exchange(tok, ctx)
    far_sum = pair_sum(far, swap(farcore, "core"))
    rows = token_rows(sc, tok_in, mixed)
    grads = last_sum(dq, own, swap(core_part, "core"), mirror(far_sum))
    recvs = [rows] + [shift(rows, -n) for n in range(1, NDP)]
    image_grads = image_out(
        sc, owner, recvs, key_weight, value_weight, image_embed, norm_scale
    )
    query_grads, key_grads, value_grads = unpack(half, exchange(grads, ("y", "zl")))
    return (query_grads[None], key_grads[None], value_grads[None], image_grads)


def solution(mesh):
    ctx = ("y", "zh", "zl", "core")
    split = Mesh(mesh.devices.reshape(4, 4, 2, 2, 2), ("dp",) + ctx)
    rows = P("dp", ctx, None)
    image = P(None, ctx, "dp")
    in_specs = (rows, rows, rows, rows, P("dp"), P("dp"), P(), P(), P(), P("dp"), image)
    out_specs = (rows, rows, rows, image)
    return jax.shard_map(local, mesh=split, in_specs=in_specs, out_specs=out_specs, check_vma=False)
```

```python
import functools
import math

import jax
import jax.numpy as jnp
from jax import lax
from jax.experimental import pallas as pl
from jax.experimental.pallas import tpu as pltpu
from jax.sharding import Mesh, PartitionSpec as P

D = 4608
HD = 128
KVH = 8
TOK = 128
SLOTS = 64
NDP = 4
FS = D // NDP
SEG = 512
NSEG = 8

score_scale = 144.0 ** (-0.5)
soft_cap = 50.0
norm_eps = 1e-06
tanh_scale = score_scale / soft_cap
exp2_scale = soft_cap * math.log2(math.e)

f32 = jnp.float32
bf16 = jnp.bfloat16
VM = pl.BlockSpec(memory_space=pltpu.VMEM)
ANY = pl.BlockSpec(memory_space=pl.ANY)
SM = pl.BlockSpec(memory_space=pltpu.SMEM)
NT = (((1,), (1,)), ((), ()))
NN = (((1,), (0,)), ((), ()))


def mm(a, b, dims=NN):
    return lax.dot_general(a, b, dims, preferred_element_type=f32)


def split3(x):
    hi = x.astype(bf16)
    rest = x - hi.astype(f32)
    mid = rest.astype(bf16)
    lo = (rest - mid.astype(f32)).astype(bf16)
    return hi, mid, lo


def params(mib):
    return pltpu.CompilerParams(vmem_limit_bytes=mib << 20)


def cost(us, flops=0):
    return pl.CostEstimate(flops=flops, bytes_accessed=int(us * 3_000_000), transcendentals=0)


def pack_kernel(width, half_ref, a_ref, b_ref, out_ref):
    for h in range(KVH):
        at = (h // 2) * 2 + (h % 2 + half_ref[0] - 2 * (h % 2) * half_ref[0])
        out_ref[at, :, :width] = a_ref[:, h * width : (h + 1) * width]
        out_ref[at, :, width:] = b_ref[:, h * width : (h + 1) * width]


def pack_heads(half, a, b, name):
    width = a.shape[1] // KVH
    return pl.pallas_call(
        functools.partial(pack_kernel, width),
        out_shape=jax.ShapeDtypeStruct((KVH, TOK, 2 * width), bf16),
        in_specs=[SM, VM, VM],
        out_specs=VM,
        compiler_params=params(60),
        cost_estimate=cost(2),
        name=name,
    )(half, a, b)


def mixed_kernel(
    sc_ref, owner_ref, embed_ref, scale_ref, wk_ref, wv_ref, mark_ref, u0, u1, u2, u3, wk_s, wv_s, sems
):
    at = pl.ds(pl.multiple_of(sc_ref[5] * FS, FS), FS)
    copies = (
        pltpu.make_async_copy(wk_ref.at[at], wk_s, sems.at[0]),
        pltpu.make_async_copy(wv_ref.at[at], wv_s, sems.at[1]),
    )
    for copy in copies:
        copy.start()
    mark_ref[...] = jnp.zeros_like(mark_ref)
    lane = lax.broadcasted_iota(jnp.int32, (SLOTS, 128), 1)
    scale = scale_ref[...].reshape(1, FS)
    outs = (u0, u1, u2, u3)
    scaled = []
    for n in range(NDP):
        rows = embed_ref[owner_ref[n]].astype(f32)
        tail = jnp.zeros((SLOTS, 128), f32)
        for k, part in enumerate(split3(jnp.sum(rows * rows, 1, keepdims=True))):
            tail = jnp.where(lane == k, part.astype(f32), tail)
        outs[n][:, 2 * KVH * HD :] = tail.astype(bf16)
        scaled.append((rows * scale).astype(bf16))
    scaled = jnp.concatenate(scaled, 0)
    for half, (copy, w_s) in enumerate(zip(copies, (wk_s, wv_s))):
        copy.wait()
        mixed = mm(scaled, w_s[...]).astype(bf16)
        for n in range(NDP):
            outs[n][:, half * KVH * HD : (half + 1) * KVH * HD] = mixed[
                n * SLOTS : (n + 1) * SLOTS
            ]


def mix(sc, owner, embed, scale, wk, wv):
    one = jax.ShapeDtypeStruct((SLOTS, 2 * KVH * HD + 128), bf16)
    return pl.pallas_call(
        mixed_kernel,
        out_shape=(jax.ShapeDtypeStruct((8, 128), f32),) + (one,) * NDP,
        in_specs=[SM, SM, VM, VM, ANY, ANY],
        out_specs=(VM,) * (NDP + 1),
        scratch_shapes=[
            pltpu.VMEM((FS, KVH * HD), bf16),
            pltpu.VMEM((FS, KVH * HD), bf16),
            pltpu.SemaphoreType.DMA((2,)),
        ],
        compiler_params=params(60),
        cost_estimate=cost(5),
        name="mix",
    )(sc, owner, embed, scale, wk, wv)


def join(x, *after):
    return pl.pallas_call(
        lambda *refs: None,
        out_shape=jax.ShapeDtypeStruct(x.shape, x.dtype),
        in_specs=[ANY] * (1 + len(after)),
        out_specs=ANY,
        input_output_aliases={0: 0},
        compiler_params=params(2),
        cost_estimate=cost(1),
        name="join",
    )(x, *after)


def attention_kernel(
    sc_ref,
    qd_in,
    kv0_in,
    kv1_in,
    kv2_in,
    kv3_in,
    dq_ref,
    own_ref,
    core_ref,
    far_ref,
    farcore_ref,
    tok_ref,
    k_s,
    v_s,
    kt_s,
    q_s,
    do_s,
    e_s,
    w_s,
    p_s,
    dk_s,
    dv_s,
    tot,
    mom,
    dqt,
    perm,
    dot_s,
    qd_ref,
    kv_s,
    sems,
):
    prefix, zh, core = sc_ref[0], sc_ref[1], sc_ref[2]
    copies = [
        pltpu.make_async_copy(ref, kv_s.at[n], sems.at[n])
        for n, ref in enumerate((kv0_in, kv1_in, kv2_in, kv3_in))
    ]
    copies.append(pltpu.make_async_copy(qd_in, qd_ref, sems.at[4]))
    for copy in copies:
        copy.start()
    dk_s[...] = jnp.zeros_like(dk_s)
    dv_s[...] = jnp.zeros_like(dv_s)
    eye = (
        lax.broadcasted_iota(jnp.int32, (HD, HD), 0) == lax.broadcasted_iota(jnp.int32, (HD, HD), 1)
    ).astype(bf16)
    out = lax.broadcasted_iota(jnp.int32, (SEG, SEG), 0)
    src = lax.broadcasted_iota(jnp.int32, (SEG, SEG), 1)
    slot = out % 16
    c_of = (slot // 4) % 2
    want = (
        (c_of + core - 2 * c_of * core) * 256 + (slot // 8) * TOK + (slot % 4) * 32 + out // 16
    )
    perm[...] = (want == src).astype(bf16)
    for seg in range(NSEG):
        y = seg % 4
        if y == 0:
            copies[seg // 2].wait()
            copies[seg // 2 + 1].wait()
        near, away = kv_s.at[seg // 4 * 2], kv_s.at[seg // 4 * 2 + 1]
        whole = jnp.concatenate([near[2 * y], near[2 * y + 1], away[2 * y], away[2 * y + 1]], 0)
        k_s[seg] = whole[:, :HD]
        v_s[seg] = whole[:, HD:]
        kt_s[seg] = mm(eye, whole[:, :HD], NT).astype(bf16)
    copies[4].wait()

    def key_start(j):
        far = j // 4
        return (j % 4) * 1024 + (zh + far - 2 * zh * far) * SEG

    def hidden(key0, row0):
        s = lax.broadcasted_iota(jnp.int32, (SEG, SEG), 0)
        piece = s // TOK
        other = piece // 2
        key = key0 + (piece % 2) * 256 + (core + other - 2 * core * other) * TOK + s % TOK
        lane = lax.broadcasted_iota(jnp.int32, (1, SEG), 1)
        row = row0 + ((lane // TOK) % 2) * 256 + lane % TOK
        return key >= jnp.maximum(row + 1, prefix)

    def row_body(i, _):
        row0 = i * 1024 + zh * SEG + core * TOK
        limit = jnp.maximum(prefix, row0 + 384)
        full = jnp.maximum(prefix, row0 + 1)
        for head in range(2):
            for z in range(2):
                at = pl.ds((head * 2 + z) * TOK, TOK)
                q_s[at, :] = qd_ref[2 * i + z, :, head * HD : (head + 1) * HD]
                do_s[at, :] = qd_ref[2 * i + z, :, (2 + head) * HD : (3 + head) * HD]
        tot[...] = jnp.zeros_like(tot)
        mom[...] = jnp.zeros_like(mom)
        dqt[...] = jnp.zeros_like(dqt)

        def scores(y, masked):
            pair = (y, y + 4)
            for j in pair:
                for c in range(0, SEG, 256):
                    cc = slice(c, c + 256)
                    t = jnp.tanh(mm(k_s[j], q_s[cc, :], NT) * tanh_scale)
                    dp = mm(v_s[j], do_s[cc, :], NT)
                    e = jnp.exp2(t * exp2_scale)
                    if masked:
                        e = jnp.where(hidden(key_start(j), row0)[:, cc], 0.0, e)
                    tot[:, cc] += jnp.sum(e, 0, keepdims=True)
                    mom[:, cc] += jnp.sum(e * dp, 0, keepdims=True)
                    e_s[j, :, cc] = e.astype(bf16)
                    w_s[j, :, cc] = e * (1.0 - t * t)
                    p_s[j, :, cc] = dp

        def first(y, _):
            @pl.when(y * 1024 + 1024 <= full)
            def _():
                scores(y, False)

            @pl.when((y * 1024 + 1024 > full) & (y * 1024 < limit))
            def _():
                scores(y, True)

            return 0

        lax.fori_loop(0, 4, first, 0)
        inv = 1.0 / tot[...]
        delta = mom[...] * inv
        dot_s[...] = (mm(eye, do_s[...], NT) * inv).astype(bf16)

        def second(y, _):
            @pl.when(y * 1024 < limit)
            def _():
                grad = dqt[...]
                for j in (y, y + 4):
                    ds = (w_s[j] * inv * (p_s[j] - delta)).astype(bf16)
                    dv_s[j] += mm(e_s[j], dot_s[...], NT)
                    dk_s[j] += mm(ds, q_s[...])
                    grad += mm(kt_s[j], ds)
                dqt[...] = grad

            return 0

        lax.fori_loop(0, 4, second, 0)
        dq = (dqt[...] * score_scale).T.astype(bf16)
        for head in range(2):
            for z in range(2):
                at = (head * 2 + z) * TOK
                dq_ref[2 * i + z, :, head * HD : (head + 1) * HD] = dq[at : at + TOK]
        return 0

    lax.fori_loop(0, 4, row_body, 0)

    for seg in range(NSEG):
        near, away = ((own_ref, core_ref), (far_ref, farcore_ref))[seg // 4]
        y = seg % 4
        terms = jnp.concatenate([dk_s[seg] * score_scale, dv_s[seg]], 1)
        near[2 * y] = terms[:TOK].astype(near.dtype)
        near[2 * y + 1] = terms[TOK : 2 * TOK].astype(near.dtype)
        away[2 * y] = terms[2 * TOK : 3 * TOK].astype(away.dtype)
        away[2 * y + 1] = terms[3 * TOK :].astype(away.dtype)
        if y < 2:
            moved = mm(perm[...], terms.astype(bf16)).astype(bf16).reshape(32, 16, 2 * HD)
            z_at = zh if seg < 4 else 1 - zh
            tok_ref[:, pl.ds(pl.multiple_of((2 * y + z_at) * 16, 16), 16), :] = moved


def attention(sc, qd, kv0, kv1, kv2, kv3):
    part = (KVH, TOK, 2 * HD)
    return pl.pallas_call(
        attention_kernel,
        out_shape=(
            jax.ShapeDtypeStruct(part, bf16),
            jax.ShapeDtypeStruct(part, f32),
            jax.ShapeDtypeStruct(part, bf16),
            jax.ShapeDtypeStruct(part, bf16),
            jax.ShapeDtypeStruct(part, bf16),
            jax.ShapeDtypeStruct((32, SLOTS, 2 * HD), bf16),
        ),
        in_specs=[SM] + [ANY] * 5,
        out_specs=(VM,) * 6,
        scratch_shapes=[
            pltpu.VMEM((NSEG, SEG, HD), bf16),
            pltpu.VMEM((NSEG, SEG, HD), bf16),
            pltpu.VMEM((NSEG, HD, SEG), bf16),
            pltpu.VMEM((SEG, HD), bf16),
            pltpu.VMEM((SEG, HD), bf16),
            pltpu.VMEM((NSEG, SEG, SEG), bf16),
            pltpu.VMEM((NSEG, SEG, SEG), f32),
            pltpu.VMEM((NSEG, SEG, SEG), f32),
            pltpu.VMEM((NSEG, SEG, HD), f32),
            pltpu.VMEM((NSEG, SEG, HD), f32),
            pltpu.VMEM((1, SEG), f32),
            pltpu.VMEM((1, SEG), f32),
            pltpu.VMEM((HD, SEG), f32),
            pltpu.VMEM((SEG, SEG), bf16),
            pltpu.VMEM((HD, SEG), bf16),
            pltpu.VMEM((KVH, TOK, 4 * HD), bf16),
            pltpu.VMEM((4, KVH, TOK, 2 * HD), bf16),
            pltpu.SemaphoreType.DMA((5,)),
        ],
        compiler_params=params(60),
        cost_estimate=cost(36),
        name="attention",
    )(sc, qd, kv0, kv1, kv2, kv3)


def pair_sum_kernel(a_ref, b_ref, out_ref):
    out_ref[...] = (a_ref[...].astype(f32) + b_ref[...].astype(f32)).astype(bf16)


def pair_sum(a, b):
    return pl.pallas_call(
        pair_sum_kernel,
        out_shape=jax.ShapeDtypeStruct(a.shape, bf16),
        in_specs=[VM, VM],
        out_specs=VM,
        compiler_params=params(8),
        cost_estimate=cost(2, 3_000_000_000),
        name="pair_sum",
    )(a, b)


def last_sum_kernel(dq_ref, a_ref, b_ref, c_ref, out_ref):
    out_ref[:, :, : 2 * HD] = dq_ref[...]
    total = a_ref[...] + b_ref[...].astype(f32) + c_ref[...].astype(f32)
    out_ref[:, :, 2 * HD :] = total.astype(bf16)


def last_sum(dq, a, b, c):
    return pl.pallas_call(
        last_sum_kernel,
        out_shape=jax.ShapeDtypeStruct((KVH, TOK, 4 * HD), bf16),
        in_specs=[VM] * 4,
        out_specs=VM,
        compiler_params=params(8),
        cost_estimate=cost(3),
        name="last_sum",
    )(dq, a, b, c)


def unpack_kernel(half_ref, in_ref, q_ref, k_ref, v_ref):
    for h in range(KVH):
        at = (h // 2) * 2 + (h % 2 + half_ref[0] - 2 * (h % 2) * half_ref[0])
        q_ref[:, h * 2 * HD : (h + 1) * 2 * HD] = in_ref[at, :, : 2 * HD]
        k_ref[:, h * HD : (h + 1) * HD] = in_ref[at, :, 2 * HD : 3 * HD]
        v_ref[:, h * HD : (h + 1) * HD] = in_ref[at, :, 3 * HD :]


def unpack(half, grads):
    return pl.pallas_call(
        unpack_kernel,
        out_shape=(
            jax.ShapeDtypeStruct((TOK, 2 * KVH * HD), bf16),
            jax.ShapeDtypeStruct((TOK, KVH * HD), bf16),
            jax.ShapeDtypeStruct((TOK, KVH * HD), bf16),
        ),
        in_specs=[SM, VM],
        out_specs=(VM, VM, VM),
        compiler_params=params(8),
        cost_estimate=cost(2),
        name="unpack",
    )(half, grads)


def token_kernel(sc_ref, tok_ref, u0, u1, u2, u3, out_ref):
    token = lax.broadcasted_iota(jnp.int32, (SLOTS, 2 * HD), 0) * 32 + sc_ref[4]
    visible = token < sc_ref[3]
    wide = KVH * HD
    cross = jnp.zeros((SLOTS, 1), f32)
    for h in range(KVH):
        base = (h // 2) * 8 + (h % 2) * 2
        away = (h // 2) * 8 + 4 + (1 - h % 2) * 2
        total = tok_ref[base].astype(f32) + tok_ref[base + 1].astype(f32)
        total = total + tok_ref[away].astype(f32) + tok_ref[away + 1].astype(f32)
        total = jnp.where(visible, total, 0.0).astype(bf16)
        for half in range(2):
            at = slice(half * wide + h * HD, half * wide + (h + 1) * HD)
            part = total[:, half * HD : (half + 1) * HD]
            out_ref[:, at] = part
            mixed = u0[:, at].astype(f32) + u1[:, at].astype(f32)
            mixed = mixed + u2[:, at].astype(f32) + u3[:, at].astype(f32)
            cross += jnp.sum(part.astype(f32) * mixed, 1, keepdims=True)
    lane = lax.broadcasted_iota(jnp.int32, (SLOTS, 128), 1)
    tail = u0[:, 2 * wide :].astype(f32) + u1[:, 2 * wide :].astype(f32)
    tail = tail + u2[:, 2 * wide :].astype(f32) + u3[:, 2 * wide :].astype(f32)
    sq = jnp.sum(tail, 1, keepdims=True)
    parts = split3(lax.rsqrt(sq / D + norm_eps)) + split3(cross / D)
    tail = jnp.zeros((SLOTS, 128), f32)
    for n, part in enumerate(parts):
        tail = jnp.where(lane == n, part.astype(f32), tail)
    out_ref[:, 2 * wide :] = tail.astype(bf16)


def token_rows(sc, tok, mixed):
    return pl.pallas_call(
        token_kernel,
        out_shape=jax.ShapeDtypeStruct((SLOTS, 2 * KVH * HD + 128), bf16),
        in_specs=[SM] + [VM] * 5,
        out_specs=VM,
        compiler_params=params(60),
        cost_estimate=cost(2),
        name="token_rows",
    )(sc, tok, *mixed)


def image_kernel(
    sc_ref, owner_ref, r0, r1, r2, r3, wk_ref, wv_ref, embed_ref, scale_ref, out_ref, wk_s, wv_s, sems
):
    at = pl.ds(pl.multiple_of(sc_ref[5] * FS, FS), FS)
    copies = (
        pltpu.make_async_copy(wk_ref.at[at], wk_s, sems.at[0]),
        pltpu.make_async_copy(wv_ref.at[at], wv_s, sems.at[1]),
    )
    for copy in copies:
        copy.start()
    wide = KVH * HD
    recvs = (r0, r1, r2, r3)
    xk = jnp.concatenate([r[:, :wide] for r in recvs], 0)
    xv = jnp.concatenate([r[:, wide : 2 * wide] for r in recvs], 0)
    copies[0].wait()
    projected = mm(xk, wk_s[...], NT)
    copies[1].wait()
    projected = projected + mm(xv, wv_s[...], NT)
    lane = lax.broadcasted_iota(jnp.int32, (SLOTS, 128), 1)
    scale = scale_ref[...].reshape(1, FS)
    for n, recv_ref in enumerate(recvs):
        row = owner_ref[n]
        tail = recv_ref[:, 2 * wide :].astype(f32)
        inv = jnp.sum(jnp.where(lane < 3, tail, 0.0), 1, keepdims=True)
        cross = jnp.sum(jnp.where(lane >= 3, tail, 0.0), 1, keepdims=True)
        grad = projected[n * SLOTS : (n + 1) * SLOTS].astype(bf16).astype(f32)
        rows = embed_ref[row].astype(f32)
        out_ref[row] = inv * (scale * grad) - rows * (inv * inv * inv * cross)


def image_out(sc, owner, recvs, wk, wv, embed, scale):
    return pl.pallas_call(
        image_kernel,
        out_shape=jax.ShapeDtypeStruct((NDP, SLOTS, FS), f32),
        in_specs=[SM, SM] + [VM] * 4 + [ANY, ANY, VM, VM],
        out_specs=VM,
        scratch_shapes=[
            pltpu.VMEM((FS, KVH * HD), bf16),
            pltpu.VMEM((FS, KVH * HD), bf16),
            pltpu.SemaphoreType.DMA((2,)),
        ],
        compiler_params=params(60),
        cost_estimate=cost(5, 60_000_000_000),
        name="image_out",
    )(sc, owner, *recvs, wk, wv, embed, scale)


def exchange(x, axes):
    return lax.all_to_all(x, axes, split_axis=0, concat_axis=0, tiled=True)


def shift(x, by):
    return lax.ppermute(x, "dp", [(i, (i + by) % NDP) for i in range(NDP)])


def mirror(x):
    return lax.ppermute(x, ("zh", "zl"), [(i, 3 - i) for i in range(4)])


def swap(x, axis):
    return lax.ppermute(x, axis, [(0, 1), (1, 0)])


def local(
    query_states,
    key_states,
    value_states,
    out_grads,
    image_counts,
    prefix_lengths,
    encoder_owner,
    key_weight,
    value_weight,
    norm_scale,
    image_embed,
):
    ctx = ("y", "zh", "zl", "core")
    dp = lax.axis_index("dp")
    half = lax.axis_index("zh").astype(jnp.int32).reshape(1)
    sc = jnp.stack(
        [
            prefix_lengths[0],
            lax.axis_index("zh"),
            lax.axis_index("core"),
            image_counts[0],
            lax.axis_index(ctx),
            dp,
        ]
    ).astype(jnp.int32)
    owner = lax.dynamic_slice(jnp.concatenate([encoder_owner, encoder_owner]), (dp,), (NDP,))

    kv0 = exchange(pack_heads(half, key_states[0], value_states[0], "pack_kv"), ("y", "zl"))
    qd_pack = pack_heads(half, query_states[0], out_grads[0], "pack_qd")
    mark, *mixed = mix(sc, owner, image_embed, norm_scale, key_weight, value_weight)
    kv0 = join(kv0, mark, qd_pack)
    kv1 = swap(kv0, "core")
    mixed = [mixed[0]] + [shift(mixed[n], n) for n in range(1, NDP)]
    kv2 = join(mirror(kv0), mixed[1], mixed[3])
    kv3 = swap(kv2, "core")
    qd = exchange(qd_pack, ("y", "zl"))

    dq, own, core_part, far, farcore, tok = attention(sc, qd, kv0, kv1, kv2, kv3)

    tok_in = exchange(tok, ctx)
    far_sum = pair_sum(far, swap(farcore, "core"))
    rows = token_rows(sc, tok_in, mixed)
    grads = last_sum(dq, own, swap(core_part, "core"), mirror(far_sum))
    recvs = [rows] + [shift(rows, -n) for n in range(1, NDP)]
    image_grads = image_out(
        sc, owner, recvs, key_weight, value_weight, image_embed, norm_scale
    )
    query_grads, key_grads, value_grads = unpack(half, exchange(grads, ("y", "zl")))
    return (query_grads[None], key_grads[None], value_grads[None], image_grads)


def solution(mesh):
    ctx = ("y", "zh", "zl", "core")
    split = Mesh(mesh.devices.reshape(4, 4, 2, 2, 2), ("dp",) + ctx)
    rows = P("dp", ctx, None)
    image = P(None, ctx, "dp")
    in_specs = (rows, rows, rows, rows, P("dp"), P("dp"), P(), P(), P(), P("dp"), image)
    out_specs = (rows, rows, rows, image)
    return jax.shard_map(local, mesh=split, in_specs=in_specs, out_specs=out_specs, check_vma=False)
```
